32 devices in a mesh: surf: 8 (over z, y), depth: 4 (over x, core).
Axes of the slice: x: 2, y: 2, z: 4, core: 2. Of those that a mesh axis runs over, the one named last changes fastest.
Arguments:
- wave_now: float32 [4, 64, 64, 128], P(None, 'surf', 'depth'), may hold values from -6 to 6
- wave_old: float32 [4, 64, 64, 128], P(None, 'surf', 'depth'), may hold values from -6 to 6
- adj_now: float32 [4, 64, 64, 128], P(None, 'surf', 'depth'), may hold values from -6 to 6
- adj_old: float32 [4, 64, 64, 128], P(None, 'surf', 'depth'), may hold values from -6 to 6
- source: float32 [4, 64, 64, 128], P(None, 'surf', 'depth'), may hold values from -24 to 24
- adj_source: float32 [4, 64, 64, 128], P(None, 'surf', 'depth'), may hold values from -24 to 24
- inv_density: float32 [125, 8192], P(None, ('surf', 'depth')), may hold values from 0.5 to 1.5
- inv_modulus: float32 [125, 8192], P(None, ('surf', 'depth')), may hold values from 0.5 to 1.5
- element_cell: int32 [32, 256], P(('surf', 'depth')), may hold values from 0 to 255, as said below
- send_elem: int32 [32, 4, 256], P(('surf', 'depth')), may hold values from 0 to 255, as said below
- send_brick: int32 [32, 4, 256], P(('surf', 'depth')), may hold values from 0 to 1023, as said below
- send_count: int32 [32, 4], P(('surf', 'depth')), may hold values from 0 to 256, as said below
Outputs:
- wave_next: float32 [4, 64, 64, 128], P(None, 'surf', 'depth')
- adj_next: float32 [4, 64, 64, 128], P(None, 'surf', 'depth')
- brick_kernel: float32 [125, 32768], P(None, ('surf', 'depth'))
The draws below stay inside these ranges and needn't reach their ends.
Inputs may be any that keep to these rules, and one draw needn't show every extreme that they name: Each row of element_cell is a permutation of the cells of one device. `send_elem`: row t of device k lists in its first send_count[k, t] slots the stored elements of device k whose blocks go to row t's device; over the four rows of a device each of its elements is listed exactly once; other slots hold 0. `send_brick`: in live slots the receiving brick within the receiving device; other slots hold 0. `send_count`: A device's counts sum to 256; rows 1 and 3 of devices with the last surf index, and rows 2 and 3 of devices with the last depth index, are empty; in every draw the device with the last surf and depth index fills row 0 with all 256 slots.
All inputs are finite; a program needn't handle non-finite values.
Results may differ from the reference program's by a relative error of at most 0.0003.
Values sent between devices are 32-bit elements; how exact they have to be, the bound alone decides.
A program may use at most 128 MiB of HBM per device.

```python
import math
import jax
import jax.numpy as jnp
import numpy as np
from jax import lax

SHOTS = 4
GLL_NODES = 125
ELEM_A = 2
ELEM_C = 4
ELEM_B = 32
BRICK_DEV = 1024
ELEM_DEV = 256
ELEMS = 8192
NODES_A = 8
NODES_C = 16
NODES_B = 128
GRID_A = 64
GRID_C = 64
SLOTS = 256
BRICKS = 32768
N_SURF = 8
N_DEPTH = 4
DEVICES = 32


def route_tables(key):
    base_key = jax.random.fold_in(key, 4242)
    cut_a = jax.random.randint(jax.random.fold_in(base_key, 1), (N_SURF,), 0, ELEM_A + 1).astype(jnp.int32)
    cut_a = jnp.where(jnp.arange(N_SURF) == N_SURF - 1, ELEM_A, cut_a).astype(jnp.int32)
    cut_c = jax.random.randint(jax.random.fold_in(base_key, 2), (N_DEPTH,), 0, ELEM_C + 1).astype(jnp.int32)
    cut_c = jnp.where(jnp.arange(N_DEPTH) == N_DEPTH - 1, ELEM_C, cut_c).astype(jnp.int32)

    def one_source(source_key, device):
        subkeys = jax.random.split(source_key, 3)
        surf_index = device // N_DEPTH
        depth_index = device % N_DEPTH
        cells = jax.random.permutation(subkeys[0], ELEM_DEV).astype(jnp.int32)
        cell_a = cells // (ELEM_C * ELEM_B)
        cell_c = cells // ELEM_B % ELEM_C
        target_row = (cell_a >= cut_a[surf_index]).astype(jnp.int32) + 2 * (cell_c >= cut_c[depth_index]).astype(jnp.int32)
        stored = jnp.arange(ELEM_DEV, dtype=jnp.int32)
        ranking = jnp.argsort(target_row, stable=True)
        sorted_row = target_row[ranking]
        counts = jnp.sum((target_row[:, None] == jnp.arange(4, dtype=jnp.int32)[None, :]).astype(jnp.int32), 0)
        starts = jnp.cumsum(counts) - counts
        slot_rank = stored - starts[sorted_row]
        element_lists = jnp.zeros((4, SLOTS), jnp.int32).at[sorted_row, slot_rank].set(stored[ranking])
        bricks = jax.random.randint(subkeys[2], (4, SLOTS), 0, BRICK_DEV).astype(jnp.int32)
        live_slot = jnp.arange(SLOTS, dtype=jnp.int32)[None, :] < counts[:, None]
        bricks = jnp.where(live_slot, bricks, 0).astype(jnp.int32)
        return (cells, element_lists, bricks, counts.astype(jnp.int32))
    source_keys = jax.random.split(jax.random.fold_in(base_key, 3), DEVICES)
    return jax.vmap(one_source)(source_keys, jnp.arange(DEVICES, dtype=jnp.int32))


def draw_element_cell(key, part):
    return route_tables(key)[0]


def draw_send_elem(key, part):
    return route_tables(key)[1]


def draw_send_brick(key, part):
    return route_tables(key)[2]


def draw_send_count(key, part):
    return route_tables(key)[3]


def shard_levels(key, dims, cuts, smallest, largest):
    factor_of = 1.0
    for dim, blocks in cuts:
        heights = jax.random.uniform(jax.random.fold_in(jax.random.fold_in(key, 6), dim), (blocks,), jnp.float32, smallest / len(cuts), largest / len(cuts))
        factor_of = factor_of * jnp.repeat(jnp.exp(heights), dims[dim] // blocks).reshape((-1,) + (1,) * (len(dims) - 1 - dim))
    return factor_of


def gaussian(rng, dims, width, limit, cuts=(), kind=jnp.bfloat16):
    result = width * jax.random.normal(rng, dims, jnp.float32)
    if cuts:
        result = result * shard_levels(rng, dims, cuts, -0.22, 0.18)
    return jnp.clip(result, -limit, limit).astype(kind)


def setup_inputs(seed: int = 0) -> dict:
    arg_keys = jax.random.split(jax.random.key(seed), 13)
    wave_now = gaussian(arg_keys[0], (SHOTS, GRID_A, GRID_C, NODES_B), 1.0, 6.0, ((1, 8), (2, 4)), jnp.float32)
    wave_old = gaussian(arg_keys[1], (SHOTS, GRID_A, GRID_C, NODES_B), 1.0, 6.0, ((1, 8), (2, 4)), jnp.float32)
    adj_now = gaussian(arg_keys[2], (SHOTS, GRID_A, GRID_C, NODES_B), 1.0, 6.0, ((1, 8), (2, 4)), jnp.float32)
    adj_old = gaussian(arg_keys[3], (SHOTS, GRID_A, GRID_C, NODES_B), 1.0, 6.0, ((1, 8), (2, 4)), jnp.float32)
    source = gaussian(arg_keys[4], (SHOTS, GRID_A, GRID_C, NODES_B), 4.0, 24.0, ((1, 8), (2, 4)), jnp.float32)
    adj_source = gaussian(arg_keys[5], (SHOTS, GRID_A, GRID_C, NODES_B), 4.0, 24.0, ((1, 8), (2, 4)), jnp.float32)
    inv_density = jnp.clip(jnp.exp(math.log(1.5) - 1.0986123 * jax.random.uniform(arg_keys[6], (GLL_NODES, ELEMS), jnp.float32) ** shard_levels(arg_keys[6], (GLL_NODES, ELEMS), ((1, 32),), -0.2, 0.2)), 0.5, 1.5)
    inv_modulus = jnp.clip(jnp.exp(math.log(1.5) - 1.0986123 * jax.random.uniform(arg_keys[7], (GLL_NODES, ELEMS), jnp.float32) ** shard_levels(arg_keys[7], (GLL_NODES, ELEMS), ((1, 32),), -0.2, 0.2)), 0.5, 1.5)
    element_cell = draw_element_cell(jax.random.fold_in(arg_keys[12], 71), 0)
    send_elem = draw_send_elem(jax.random.fold_in(arg_keys[12], 71), 0)
    send_brick = draw_send_brick(jax.random.fold_in(arg_keys[12], 71), 0)
    send_count = draw_send_count(jax.random.fold_in(arg_keys[12], 71), 0)
    return {"wave_now": wave_now, "wave_old": wave_old, "adj_now": adj_now, "adj_old": adj_old, "source": source, "adj_source": adj_source, "inv_density": inv_density, "inv_modulus": inv_modulus, "element_cell": element_cell, "send_elem": send_elem, "send_brick": send_brick, "send_count": send_count}


time_step = 0.05
precise = lax.Precision.HIGHEST

def gll_tables():
    points = np.array([-1.0, -math.sqrt(3.0 / 7.0), 0.0, math.sqrt(3.0 / 7.0), 1.0])
    weights = np.array([0.1, 49.0 / 90.0, 32.0 / 45.0, 49.0 / 90.0, 0.1])
    identity = np.eye(5)
    on_diagonal = identity > 0.5
    differences = points[:, None] - points[None, :] + identity
    products = np.prod(differences, axis=1)
    derivative = products[:, None] / products[None, :] / differences
    inverse = np.where(on_diagonal, 0.0, 1.0 / differences)
    derivative = np.where(on_diagonal, inverse.sum(axis=1)[:, None], derivative)
    return (jnp.asarray(derivative, jnp.float32), jnp.asarray(weights, jnp.float32))

def node_ids(cell_ids):
    cell_a = cell_ids // (ELEM_C * ELEM_B)
    cell_c = cell_ids // ELEM_B % ELEM_C
    cell_b = cell_ids % ELEM_B
    local_ids = jnp.arange(GLL_NODES, dtype=jnp.int32)
    along_a = local_ids // 25
    along_c = local_ids // 5 % 5
    along_b = local_ids % 5
    node_a = 4 * cell_a[None, :] + along_a[:, None]
    node_c = 4 * cell_c[None, :] + along_c[:, None]
    node_b = (4 * cell_b[None, :] + along_b[:, None]) % (4 * ELEM_B)
    return ((node_a * (4 * ELEM_C + 1) + node_c) * (4 * ELEM_B) + node_b).astype(jnp.int32)

def element_terms(values, density, modulus, shot_count):
    derivative, weights = gll_tables()
    cubature = weights[:, None, None] * weights[None, :, None] * weights[None, None, :]
    elem_count = values.shape[-1]
    nodal = values.reshape(values.shape[0], 5, 5, 5, elem_count)
    grad_a = jnp.einsum('ip,xpqre->xiqre', derivative, nodal, precision=precise)
    grad_c = jnp.einsum('jq,xpqre->xpjre', derivative, nodal, precision=precise)
    grad_b = jnp.einsum('kr,xpqre->xpqke', derivative, nodal, precision=precise)
    stiffness = cubature[..., None] * density.reshape(5, 5, 5, elem_count)
    forces = jnp.einsum('ip,xiqre->xpqre', derivative, stiffness * grad_a, precision=precise) + jnp.einsum('jq,xpjre->xpqre', derivative, stiffness * grad_c, precision=precise) + jnp.einsum('kr,xpqke->xpqre', derivative, stiffness * grad_b, precision=precise)
    lumped_mass = cubature[..., None] * modulus.reshape(5, 5, 5, elem_count)
    product = grad_a[:shot_count] * grad_a[shot_count:] + grad_c[:shot_count] * grad_c[shot_count:] + grad_b[:shot_count] * grad_b[shot_count:]
    kernel = -time_step * cubature[..., None] * lax.optimization_barrier(jnp.sum(product, axis=0))
    partial_value = jnp.concatenate([forces.reshape(2 * shot_count, GLL_NODES, elem_count), lumped_mass.reshape(1, GLL_NODES, elem_count)], 0)
    return (partial_value, kernel.reshape(GLL_NODES, elem_count))

def reference(wave_now, wave_old, adj_now, adj_old, source, adj_source, inv_density, inv_modulus, element_cell, send_elem, send_brick, send_count):
    fields = jnp.concatenate([wave_now, adj_now], 0)
    padded = jnp.pad(fields, ((0, 0), (0, 1), (0, 1), (0, 0)))
    channels = 2 * SHOTS + 1
    global_sum = jnp.zeros((channels, GRID_A + 1, GRID_C + 1, NODES_B), jnp.float32)

    def one_device(global_sum, device):
        surf_index = device // N_DEPTH
        depth_index = device % N_DEPTH
        start_a = (surf_index * NODES_A).astype(jnp.int32)
        start_c = (depth_index * NODES_C).astype(jnp.int32)
        zero_index = jnp.zeros((), jnp.int32)
        corner = (zero_index, start_a, start_c, zero_index)
        block = lax.dynamic_slice(padded, corner, (2 * SHOTS, NODES_A + 1, NODES_C + 1, NODES_B))
        flattened = block.reshape(2 * SHOTS, -1)
        cell_ids = lax.dynamic_index_in_dim(element_cell, device, 0, keepdims=False)
        node_map = node_ids(cell_ids)
        values = jnp.take(flattened, node_map, axis=1)
        column = (device * ELEM_DEV).astype(jnp.int32)
        density = lax.dynamic_slice_in_dim(inv_density, column, ELEM_DEV, 1)
        modulus = lax.dynamic_slice_in_dim(inv_modulus, column, ELEM_DEV, 1)
        partial_value, kernel = element_terms(values, density, modulus, SHOTS)
        assembled_local = jnp.zeros((channels, flattened.shape[1]), jnp.float32)
        assembled_local = assembled_local.at[:, node_map.reshape(-1)].add(partial_value.reshape(channels, -1))
        assembled_local = assembled_local.reshape(channels, NODES_A + 1, NODES_C + 1, NODES_B)
        current = lax.dynamic_slice(global_sum, corner, assembled_local.shape)
        global_sum = lax.dynamic_update_slice(global_sum, current + assembled_local, corner)
        return (global_sum, kernel)
    global_sum, kernels = lax.scan(one_device, global_sum, jnp.arange(DEVICES, dtype=jnp.int32))
    assembled = global_sum[:, :GRID_A, :GRID_C, :]
    lumped_mass = assembled[2 * SHOTS:]
    step_square = time_step * time_step
    wave_next = 2.0 * wave_now - wave_old + step_square * (source - assembled[:SHOTS]) / lumped_mass
    adj_next = 2.0 * adj_now - adj_old + step_square * (adj_source - assembled[SHOTS:2 * SHOTS]) / lumped_mass
    kernel_all = kernels.transpose(1, 0, 2).reshape(GLL_NODES, ELEMS)
    slot_ids = jnp.arange(SLOTS, dtype=jnp.int32)
    live_slot = slot_ids[None, None, :] < send_count[:, :, None]
    source_dev = jnp.arange(DEVICES, dtype=jnp.int32)[:, None, None]
    row_ids = jnp.arange(4, dtype=jnp.int32)[None, :, None]
    target_dev = ((source_dev // N_DEPTH + row_ids % 2) * N_DEPTH + source_dev % N_DEPTH + row_ids // 2).astype(jnp.int32)
    element_id = (source_dev * ELEM_DEV + send_elem).astype(jnp.int32)
    brick_id = jnp.where(live_slot, target_dev * BRICK_DEV + send_brick, -1).astype(jnp.int32)
    brick_of = jnp.full((ELEMS,), -1, jnp.int32).at[element_id.reshape(-1)].max(brick_id.reshape(-1))
    brick_kernel = jax.ops.segment_sum(kernel_all.T, brick_of, num_segments=BRICKS).T
    return (wave_next, adj_next, brick_kernel)
```

```python
import functools
import math

import jax
import jax.numpy as jnp
import numpy as np
from jax import lax
from jax.experimental import pallas as pl
from jax.experimental.pallas import tpu as pltpu
from jax.sharding import PartitionSpec as P

time_step = 0.05
precise = lax.Precision.HIGHEST
MESH = pl.DeviceIdType.MESH
f32 = jnp.float32
bf16 = jnp.bfloat16

NODES_A, NODES_C, NODES_B = 8, 16, 128
PLANE = NODES_A * NODES_C
BLOCK_ROWS = 144
FACE_A, FACE_C, FACE_D = 144, 72, 16


def gll_numbers():
    points = np.array([-1.0, -math.sqrt(3.0 / 7.0), 0.0, math.sqrt(3.0 / 7.0), 1.0])
    weights = np.array([0.1, 49.0 / 90.0, 32.0 / 45.0, 49.0 / 90.0, 0.1])
    identity = np.eye(5)
    on_diagonal = identity > 0.5
    differences = points[:, None] - points[None, :] + identity
    products = np.prod(differences, axis=1)
    derivative = products[:, None] / products[None, :] / differences
    inverse = np.where(on_diagonal, 0.0, 1.0 / differences)
    derivative = np.where(on_diagonal, inverse.sum(axis=1)[:, None], derivative)
    return derivative, weights


D, W = gll_numbers()


def tables():
    spread = np.zeros((512, 640), np.float32)
    for ec in range(4):
        for eb in range(32):
            for r in range(5):
                spread[ec * 128 + (4 * eb + r) % 128, r * 128 + ec * 32 + eb] = 1.0
    expand = np.zeros((1000, 128), np.float32)
    expand[np.arange(1000), np.arange(1000) // 8] = 1.0
    gather = np.zeros((128, 1024), np.float32)
    gather[np.arange(1000) // 8, np.arange(1000)] = 0.5
    select = np.zeros((480, 128), np.float32)
    for r in range(5):
        for ea in range(2):
            for p in range(5):
                for q in range(5):
                    select[(r * 2 + ea) * 48 + (4 * ea + p) * 5 + q, p * 25 + q * 5 + r] = 1.0
    cubature = (W[:, None, None] * W[None, :, None] * W[None, None, :]).reshape(-1)
    scale = np.zeros((128, 128), np.float32)
    scale[:125] = cubature[:, None]
    return (spread, spread.T.copy(), expand, gather, select), scale


def two_terms(x):
    high = x.astype(bf16)
    return high, (x - high.astype(f32)).astype(bf16)


def dot_left(x, table):
    high, low = two_terms(x)
    return jnp.dot(high, table, preferred_element_type=f32) + jnp.dot(
        low, table, preferred_element_type=f32
    )


def dot_right(table, x):
    high, low = two_terms(x)
    return jnp.dot(table, high, preferred_element_type=f32) + jnp.dot(
        table, low, preferred_element_type=f32
    )


def dot_rows(x, table):
    return lax.dot_general(x, table, (((1,), (1,)), ((), ())), preferred_element_type=f32)


def forward(v):
    s0, s1, d0, d1 = v[0] + v[4], v[1] + v[3], v[0] - v[4], v[1] - v[3]
    out = [None] * 5
    for i in range(2):
        even = (
            float((D[i, 0] + D[i, 4]) / 2) * s0
            + float((D[i, 1] + D[i, 3]) / 2) * s1
            + float(D[i, 2]) * v[2]
        )
        odd = float((D[i, 0] - D[i, 4]) / 2) * d0 + float((D[i, 1] - D[i, 3]) / 2) * d1
        out[i] = even + odd
        out[4 - i] = odd - even
    out[2] = float(D[2, 0]) * d0 + float(D[2, 1]) * d1
    return out


def backward(h):
    s0, s1, d0, d1 = h[0] + h[4], h[1] + h[3], h[0] - h[4], h[1] - h[3]
    out = [None] * 5
    for p in range(2):
        even = (
            float((D[0, p] + D[4, p]) / 2) * s0
            + float((D[1, p] + D[3, p]) / 2) * s1
            + float(D[2, p]) * h[2]
        )
        odd = float((D[0, p] - D[4, p]) / 2) * d0 + float((D[1, p] - D[3, p]) / 2) * d1
        out[p] = even + odd
        out[4 - p] = odd - even
    out[2] = float(D[0, 2]) * d0 + float(D[1, 2]) * d1
    return out


def body(
    n_surf,
    n_depth,
    wave_ref,
    adj_ref,
    density_ref,
    modulus_ref,
    cell_ref,
    elem_ref,
    brick_ref,
    count_ref,
    spread_ref,
    fold_ref,
    expand_ref,
    gather_ref,
    select_ref,
    scale_ref,
    force_ref,
    mass_ref,
    blocks_ref,
    fields,
    halo_a,
    halo_c,
    halo_d,
    stage_a,
    stage_c,
    lhs,
    values,
    stiff,
    product,
    forces,
    folded,
    mass_lhs,
    mass_fold,
    mass_sum,
    face_a,
    face_c,
    face_d,
    got_a,
    got_c,
    got_d,
    own_block,
    got_blocks,
    load_sem,
    send_sem,
    recv_sem,
):
    s = lax.axis_index("surf")
    d = lax.axis_index("depth")
    above_s, above_d = s < n_surf - 1, d < n_depth - 1
    below_s, below_d = s > 0, d > 0
    above_both, below_both = above_s & above_d, below_s & below_d
    up = ((s + 1, d, above_s), (s, d + 1, above_d), (s + 1, d + 1, above_both))
    down = ((s - 1, d, below_s), (s, d - 1, below_d), (s - 1, d - 1, below_both))

    loads = [
        pltpu.make_async_copy(wave_ref, fields.at[pl.ds(0, 4 * PLANE)], load_sem.at[0]),
        pltpu.make_async_copy(adj_ref, fields.at[pl.ds(4 * PLANE, 4 * PLANE)], load_sem.at[1]),
    ]
    for load in loads:
        load.start()
    barrier = pltpu.get_barrier_semaphore()
    for to_s, to_d, there in up + down:

        @pl.when(there)
        def _():
            pl.semaphore_signal(barrier, inc=1, device_id=(to_s, to_d), device_id_type=MESH)

    for load in loads:
        load.wait()
    for c in range(NODES_C):
        stage_a[c * 8 : c * 8 + 8, :] = fields[pl.ds(c, 8, stride=PLANE), :]
    for a in range(NODES_A):
        stage_c[a * 8 : a * 8 + 8, :] = fields[pl.ds(a * NODES_C, 8, stride=PLANE), :]
    peers = sum(there.astype(jnp.int32) for _, _, there in up + down)
    pl.semaphore_wait(barrier, peers)

    def remote(source, target, k, to):
        return pltpu.make_async_remote_copy(
            src_ref=source,
            dst_ref=target,
            send_sem=send_sem.at[k],
            recv_sem=recv_sem.at[k],
            device_id=(to[0], to[1]),
            device_id_type=MESH,
        )

    halos = [
        remote(stage_a, halo_a, 0, down[0]),
        remote(stage_c, halo_c, 1, down[1]),
        remote(stage_a.at[pl.ds(0, 8)], halo_d, 2, down[2]),
    ]
    for copy, (_, _, there) in zip(halos, down):

        @pl.when(there)
        def _():
            copy.start()

    rows = lax.broadcasted_iota(jnp.int32, (256, 256), 0)
    placing = jnp.where(cell_ref[0:1, :] == rows, 1.0, 0.0).astype(bf16)

    def to_cells(ref):
        high, low = two_terms(ref[...])
        return dot_rows(high, placing) + dot_rows(low, placing)

    scale = jnp.concatenate([scale_ref[0:125, :]] * 2, axis=1)
    density = to_cells(density_ref) * scale
    modulus = to_cells(modulus_ref) * scale
    pad = jnp.zeros((3, 256), f32)
    density = jnp.concatenate([density, pad], axis=0)
    modulus = jnp.concatenate([modulus, pad], axis=0)
    stiff[...] = dot_right(expand_ref[...], density)
    picked = dot_right(select_ref[...], modulus)
    for r in range(5):
        mass_lhs[:, r * 128 : (r + 1) * 128] = (
            picked[r * 96 : r * 96 + 48, 0:128] + picked[r * 96 + 48 : r * 96 + 96, 128:256]
        )
    mass_fold[...] = dot_left(mass_lhs[...], fold_ref[...])
    for a in range(NODES_A + 1):
        for ec in range(4):
            lanes = slice(ec * 128, ec * 128 + 128)
            mass_sum[a * 24 + 4 * ec : a * 24 + 4 * ec + 4, :] = mass_fold[a * 5 : a * 5 + 4, lanes]
        for ec in range(4):
            lanes = slice(ec * 128, ec * 128 + 128)
            tail = mass_fold[a * 5 + 4 : a * 5 + 5, lanes]
            row = a * 24 + 4 * ec + 4
            if ec < 3:
                mass_sum[row : row + 1, :] += tail
            else:
                mass_sum[row : row + 1, :] = tail

    slots = lax.broadcasted_iota(jnp.int32, (1, 256), 1)
    digit_rows = lax.broadcasted_iota(jnp.int32, (16, 256), 0)
    digits = jnp.zeros((16, 256), f32)
    for t in range(4):
        live = slots < count_ref[0, t]
        number = jnp.where(live, brick_ref[t : t + 1, :] + 1, 0)
        pair = jnp.where(
            digit_rows == 2 * t,
            number >> 5,
            jnp.where(digit_rows == 2 * t + 1, number & 31, 0),
        )
        listed = jnp.where(elem_ref[t : t + 1, :] == rows, 1.0, 0.0).astype(bf16)
        digits = digits + dot_rows(pair.astype(f32).astype(bf16), listed)
    own_block[128:144, :] = dot_rows(digits.astype(bf16), placing)

    zeros = jnp.zeros((8, 128), f32)
    lhs[360:384, :] = jnp.zeros((24, 512), f32)

    def place(a, c, tile):
        ec, q = c // 4, c % 4
        if ec < 4:
            lhs[pl.ds(pl.multiple_of((a * 5 + q) * 8, 8), 8), ec * 128 : ec * 128 + 128] = tile
        if q == 0 and ec > 0:
            lhs[pl.ds(pl.multiple_of((a * 5 + 4) * 8, 8), 8), (ec - 1) * 128 : ec * 128] = tile

    def place_plane(a, carry):
        for c in range(NODES_C):
            place(a, c, fields[pl.ds(a * NODES_C + c, 8, stride=PLANE), :])
        return carry

    lax.fori_loop(0, NODES_A, place_plane, 0)

    for buffer, (_, _, there) in zip((halo_a, halo_c, halo_d), up):

        @pl.when(jnp.logical_not(there))
        def _():
            buffer[...] = jnp.zeros(buffer.shape, f32)

    for copy, (_, _, there) in zip(halos, down):

        @pl.when(there)
        def _():
            copy.wait_send()

    for copy, (_, _, there) in zip(halos, up):

        @pl.when(there)
        def _():
            copy.wait_recv()

    for c in range(NODES_C):
        place(8, c, halo_a[c * 8 : c * 8 + 8, :])
    for a in range(NODES_A):
        place(a, 16, halo_c[a * 8 : a * 8 + 8, :])
    place(8, 16, halo_d[...])

    def spread_rows(k, carry):
        at = pl.ds(pl.multiple_of(k * 128, 128), 128)
        values[at, :] = dot_left(lhs[at, :], spread_ref[...])
        return carry

    lax.fori_loop(0, 3, spread_rows, 0)
    product[1000:1024, :] = jnp.zeros((24, 256), f32)

    def mates(g):
        return g * pltpu.roll(g, 4, 0)

    def eight(k):
        return pl.ds(pl.multiple_of(k * 8, 8), 8)

    for ea in range(2):
        half = slice(ea * 128, ea * 128 + 128)

        def plane(p, carry):
            v = [
                [
                    values[eight((4 * ea + p) * 5 + q), r * 128 : r * 128 + 128]
                    for r in range(5)
                ]
                for q in range(5)
            ]
            k = [[stiff[eight(p * 25 + q * 5 + r), half] for r in range(5)] for q in range(5)]
            pair = [[None] * 5 for _ in range(5)]
            force = [[None] * 5 for _ in range(5)]
            for r in range(5):
                g = forward([v[q][r] for q in range(5)])
                f = backward([k[q][r] * g[q] for q in range(5)])
                for q in range(5):
                    pair[q][r] = mates(g[q])
                    force[q][r] = f[q]
            for q in range(5):
                g = forward(v[q])
                f = backward([k[q][r] * g[r] for r in range(5)])
                for r in range(5):
                    product[eight(p * 25 + q * 5 + r), half] = pair[q][r] + mates(g[r])
                    forces[eight(ea * 25 + p * 5 + q), r * 128 : r * 128 + 128] = force[q][r] + f[r]
            return carry

        lax.fori_loop(0, 5, plane, 0)

        def line(q, carry):
            for r in range(5):
                lanes = slice(r * 128, r * 128 + 128)
                g = forward([values[eight((4 * ea + p) * 5 + q), lanes] for p in range(5)])
                f = backward([stiff[eight(p * 25 + q * 5 + r), half] * g[p] for p in range(5)])
                for p in range(5):
                    product[eight(p * 25 + q * 5 + r), half] += mates(g[p])
                    forces[eight(ea * 25 + p * 5 + q), lanes] += f[p]
            return carry

        lax.fori_loop(0, 5, line, 0)

    own_block[0:128, :] = dot_right(gather_ref[...], product[...]) * (
        -time_step * jnp.concatenate([scale_ref[...]] * 2, axis=1)
    )
    sends = [remote(own_block, got_blocks.at[k], 3 + k, up[k]) for k in range(3)]
    for copy, (_, _, there) in zip(sends, up):

        @pl.when(there)
        def _():
            copy.start()

    for k in range(3):

        @pl.when(jnp.logical_not(down[k][2]))
        def _():
            got_blocks[k] = jnp.zeros((BLOCK_ROWS, 256), f32)

    forces[160:200, :] += forces[200:240, :]

    def fold_rows(first, count, at):
        folded[at : at + count, :] = dot_left(forces[first : first + count, :], fold_ref[...])

    fold_rows(0, 200, 0)
    fold_rows(240, 160, 200)

    def node(a, c):
        ec, q = c // 4, c % 4
        out = None
        if ec < 4:
            out = folded[eight(a * 5 + q), ec * 128 : ec * 128 + 128]
        if q == 0 and ec > 0:
            tail = folded[eight(a * 5 + 4), (ec - 1) * 128 : ec * 128]
            out = tail if out is None else out + tail
        return out

    for c in range(NODES_C):
        face_a[c * 8 : c * 8 + 8, :] = node(8, c)
    face_a[128:144, :] = mass_sum[192:208, :]
    for a in range(NODES_A):
        face_c[a * 8 : a * 8 + 8, :] = node(a, 16)
        face_c[64 + a : 65 + a, :] = mass_sum[a * 24 + 16 : a * 24 + 17, :]
    face_d[0:8, :] = node(8, 16)
    face_d[8:16, :] = jnp.broadcast_to(mass_sum[208:209, :], (8, 128))
    faces = [
        remote(face_a, got_a, 6, up[0]),
        remote(face_c, got_c, 7, up[1]),
        remote(face_d, got_d, 8, up[2]),
    ]
    for copy, (_, _, there) in zip(faces, up):

        @pl.when(there)
        def _():
            copy.start()

    for buffer, (_, _, there) in zip((got_a, got_c, got_d), down):

        @pl.when(jnp.logical_not(there))
        def _():
            buffer[...] = jnp.zeros(buffer.shape, f32)

    def write_plane(a, carry):
        for c in range(1, NODES_C):
            force_ref[pl.ds(a * NODES_C + c, 8, stride=PLANE), :] = node(a, c)
        return carry

    lax.fori_loop(1, NODES_A, write_plane, 0)

    for copy, (_, _, there) in zip(faces, up):

        @pl.when(there)
        def _():
            copy.wait_send()

    for copy, (_, _, there) in zip(faces, down):

        @pl.when(there)
        def _():
            copy.wait_recv()

    for c in range(1, NODES_C):
        force_ref[pl.ds(c, 8, stride=PLANE), :] = node(0, c) + got_a[c * 8 : c * 8 + 8, :]
    for a in range(1, NODES_A):
        force_ref[pl.ds(a * NODES_C, 8, stride=PLANE), :] = (
            node(a, 0) + got_c[a * 8 : a * 8 + 8, :]
        )
    force_ref[pl.ds(0, 8, stride=PLANE), :] = (
        node(0, 0) + got_a[0:8, :] + got_c[0:8, :] + got_d[0:8, :]
    )
    mass_sum[0:16, :] += got_a[128:144, :]
    for a in range(NODES_A):
        mass_sum[a * 24 : a * 24 + 1, :] += got_c[64 + a : 65 + a, :]
    mass_sum[0:1, :] += got_d[8:9, :]
    for a in range(NODES_A):
        mass_ref[a * 16 : a * 16 + 16, :] = mass_sum[a * 24 : a * 24 + 16, :]

    for copy, (_, _, there) in zip(sends, up):

        @pl.when(there)
        def _():
            copy.wait_send()

    blocks_ref[0] = own_block[...]
    for k, (copy, (_, _, there)) in enumerate(zip(sends, down)):

        @pl.when(there)
        def _():
            copy.wait_recv()

        blocks_ref[1 + k] = got_blocks[k]


def per_device(
    n_surf,
    n_depth,
    wave_now,
    wave_old,
    adj_now,
    adj_old,
    source,
    adj_source,
    inv_density,
    inv_modulus,
    element_cell,
    send_elem,
    send_brick,
    send_count,
):
    constants, scale = tables()
    vmem = pl.BlockSpec(memory_space=pltpu.VMEM)
    anywhere = pl.BlockSpec(memory_space=pl.ANY)
    smem = pl.BlockSpec(memory_space=pltpu.SMEM)
    force, mass, blocks = pl.pallas_call(
        functools.partial(body, n_surf, n_depth),
        out_shape=(
            jax.ShapeDtypeStruct((8 * PLANE, 128), f32),
            jax.ShapeDtypeStruct((PLANE, 128), f32),
            jax.ShapeDtypeStruct((4, BLOCK_ROWS, 256), f32),
        ),
        in_specs=[anywhere] * 2 + [vmem] * 5 + [smem] + [vmem] * 6,
        out_specs=(vmem,) * 3,
        scratch_shapes=[
            pltpu.VMEM((8 * PLANE, 128), f32),
            pltpu.VMEM((128, 128), f32),
            pltpu.VMEM((64, 128), f32),
            pltpu.VMEM((8, 128), f32),
            pltpu.VMEM((128, 128), f32),
            pltpu.VMEM((64, 128), f32),
            pltpu.VMEM((384, 512), f32),
            pltpu.VMEM((384, 640), f32),
            pltpu.VMEM((1000, 256), f32),
            pltpu.VMEM((1024, 256), f32),
            pltpu.VMEM((400, 640), f32),
            pltpu.VMEM((360, 512), f32),
            pltpu.VMEM((48, 640), f32),
            pltpu.VMEM((48, 512), f32),
            pltpu.VMEM((216, 128), f32),
            pltpu.VMEM((FACE_A, 128), f32),
            pltpu.VMEM((FACE_C, 128), f32),
            pltpu.VMEM((FACE_D, 128), f32),
            pltpu.VMEM((FACE_A, 128), f32),
            pltpu.VMEM((FACE_C, 128), f32),
            pltpu.VMEM((FACE_D, 128), f32),
            pltpu.VMEM((BLOCK_ROWS, 256), f32),
            pltpu.VMEM((3, BLOCK_ROWS, 256), f32),
            pltpu.SemaphoreType.DMA((2,)),
            pltpu.SemaphoreType.DMA((9,)),
            pltpu.SemaphoreType.DMA((9,)),
        ],
        compiler_params=pltpu.CompilerParams(
            collective_id=0, has_side_effects=True, vmem_limit_bytes=40 * 1024 * 1024
        ),
    )(
        wave_now.reshape(4 * PLANE, 128),
        adj_now.reshape(4 * PLANE, 128),
        inv_density,
        inv_modulus,
        element_cell,
        send_elem[0],
        send_brick[0],
        send_count,
        *[jnp.asarray(c, bf16) for c in constants],
        jnp.asarray(scale, f32),
    )
    force = force.reshape(8, NODES_A, NODES_C, 128)
    mass = mass.reshape(1, NODES_A, NODES_C, 128)
    step_square = time_step * time_step
    wave_next = 2.0 * wave_now - wave_old + step_square * (source - force[:4]) / mass
    adj_next = 2.0 * adj_now - adj_old + step_square * (adj_source - force[4:]) / mass
    brick_dev = 1024
    brick_ids = jnp.arange(brick_dev, dtype=jnp.int32).astype(f32)
    brick_kernel = 0.0
    for t in range(4):
        targets = blocks[t, 128 + 2 * t] * 32.0 + blocks[t, 129 + 2 * t] - 1.0
        selector = (targets[:, None] == brick_ids[None, :]).astype(f32)
        brick_kernel = brick_kernel + jnp.dot(
            blocks[t, :125], selector, precision=precise, preferred_element_type=f32
        )
    return wave_next, adj_next, brick_kernel


def solution(mesh):
    field = P(None, "surf", "depth", None)
    column = P(None, ("surf", "depth"))
    placed = (field,) * 6 + (
        column,
        column,
        P(("surf", "depth"), None),
        P(("surf", "depth"), None, None),
        P(("surf", "depth"), None, None),
        P(("surf", "depth"), None),
    )
    return jax.shard_map(
        functools.partial(per_device, mesh.shape["surf"], mesh.shape["depth"]),
        mesh=mesh,
        in_specs=placed,
        out_specs=(field, field, column),
        check_vma=False,
    )
```

```python
import functools
import math

import jax
import jax.numpy as jnp
import numpy as np
from jax import lax
from jax.experimental import pallas as pl
from jax.experimental.pallas import tpu as pltpu
from jax.sharding import PartitionSpec as P

time_step = 0.05
MESH = pl.DeviceIdType.MESH
f32 = jnp.float32
bf16 = jnp.bfloat16

NODES_A, NODES_C, NODES_B = 8, 16, 128
PLANE = NODES_A * NODES_C
BLOCK_ROWS = 144
FACE_A, FACE_C, FACE_D = 144, 72, 16


def gll_numbers():
    points = np.array([-1.0, -math.sqrt(3.0 / 7.0), 0.0, math.sqrt(3.0 / 7.0), 1.0])
    weights = np.array([0.1, 49.0 / 90.0, 32.0 / 45.0, 49.0 / 90.0, 0.1])
    identity = np.eye(5)
    on_diagonal = identity > 0.5
    differences = points[:, None] - points[None, :] + identity
    products = np.prod(differences, axis=1)
    derivative = products[:, None] / products[None, :] / differences
    inverse = np.where(on_diagonal, 0.0, 1.0 / differences)
    derivative = np.where(on_diagonal, inverse.sum(axis=1)[:, None], derivative)
    return derivative, weights


D, W = gll_numbers()


def cubature_rows():
    cubature = (W[:, None, None] * W[None, :, None] * W[None, None, :]).reshape(-1)
    scale = np.zeros((128, 128), np.float32)
    scale[:125] = cubature[:, None]
    return scale


def iota(shape, axis):
    return lax.broadcasted_iota(jnp.int32, shape, axis)


def ones_where(condition, one=1.0):
    return jnp.where(condition, one, 0.0).astype(bf16)


def fill_tables(spread_ref, fold_ref):
    row, lane = iota((128, 128), 0), iota((128, 128), 1)
    lane_one, row_one = iota((1, 128), 1), iota((128, 1), 0)
    for ec in range(4):
        for r in range(5):
            node = jnp.where(lane_one >> 5 == ec, (4 * (lane_one & 31) + r) & 127, -1)
            spread_ref[ec * 128 : ec * 128 + 128, r * 128 : r * 128 + 128] = ones_where(row == node)
            node = jnp.where(row_one >> 5 == ec, (4 * (row_one & 31) + r) & 127, -1)
            fold_ref[r * 128 : r * 128 + 128, ec * 128 : ec * 128 + 128] = ones_where(lane == node)


def two_terms(x):
    high = x.astype(bf16)
    return high, (x - high.astype(f32)).astype(bf16)


def dot_left(x, table):
    high, low = two_terms(x)
    return jnp.dot(high, table, preferred_element_type=f32) + jnp.dot(
        low, table, preferred_element_type=f32
    )


def dot_right(table, x):
    high, low = two_terms(x)
    return jnp.dot(table, high, preferred_element_type=f32) + jnp.dot(
        table, low, preferred_element_type=f32
    )


def dot_rows(x, table):
    return lax.dot_general(x, table, (((1,), (1,)), ((), ())), preferred_element_type=f32)


def forward(v):
    s0, s1, d0, d1 = v[0] + v[4], v[1] + v[3], v[0] - v[4], v[1] - v[3]
    out = [None] * 5
    for i in range(2):
        even = (
            float((D[i, 0] + D[i, 4]) / 2) * s0
            + float((D[i, 1] + D[i, 3]) / 2) * s1
            + float(D[i, 2]) * v[2]
        )
        odd = float((D[i, 0] - D[i, 4]) / 2) * d0 + float((D[i, 1] - D[i, 3]) / 2) * d1
        out[i] = even + odd
        out[4 - i] = odd - even
    out[2] = float(D[2, 0]) * d0 + float(D[2, 1]) * d1
    return out


def backward(h):
    s0, s1, d0, d1 = h[0] + h[4], h[1] + h[3], h[0] - h[4], h[1] - h[3]
    out = [None] * 5
    for p in range(2):
        even = (
            float((D[0, p] + D[4, p]) / 2) * s0
            + float((D[1, p] + D[3, p]) / 2) * s1
            + float(D[2, p]) * h[2]
        )
        odd = float((D[0, p] - D[4, p]) / 2) * d0 + float((D[1, p] - D[3, p]) / 2) * d1
        out[p] = even + odd
        out[4 - p] = odd - even
    out[2] = float(D[0, 2]) * d0 + float(D[1, 2]) * d1
    return out


def body(
    n_surf,
    n_depth,
    wave_hbm,
    adj_hbm,
    cell_hbm,
    elem_hbm,
    brick_hbm,
    count_hbm,
    density_hbm,
    modulus_hbm,
    scale_hbm,
    wave_old_hbm,
    adj_old_hbm,
    source_hbm,
    adj_source_hbm,
    wave_out,
    adj_out,
    brick_out,
    next_ref,
    blocks_ref,
    bricks,
    fields,
    cell_ref,
    elem_ref,
    brick_ref,
    count_ref,
    density_ref,
    modulus_ref,
    scale_ref,
    fold_ref,
    spread_ref,
    old,
    driven,
    halo_a,
    halo_c,
    halo_d,
    stage_a,
    stage_c,
    lhs,
    values,
    stiff,
    product,
    forces,
    folded,
    mass_lhs,
    mass_fold,
    mass_sum,
    face_a,
    face_c,
    face_d,
    got_a,
    got_c,
    got_d,
    write_sem,
    load_sem,
    send_sem,
    recv_sem,
):
    s = lax.axis_index("surf")
    d = lax.axis_index("depth")
    above_s, above_d = s < n_surf - 1, d < n_depth - 1
    below_s, below_d = s > 0, d > 0
    above_both, below_both = above_s & above_d, below_s & below_d
    up = ((s + 1, d, above_s), (s, d + 1, above_d), (s + 1, d + 1, above_both))
    down = ((s - 1, d, below_s), (s, d - 1, below_d), (s - 1, d - 1, below_both))

    first, second = pl.ds(0, 4 * PLANE), pl.ds(4 * PLANE, 4 * PLANE)
    moves = [
        (wave_hbm, fields.at[first]),
        (adj_hbm, fields.at[second]),
        (cell_hbm, cell_ref),
        (density_hbm, density_ref),
        (modulus_hbm, modulus_ref),
        (scale_hbm, scale_ref),
        (elem_hbm, elem_ref),
        (brick_hbm, brick_ref),
        (count_hbm, count_ref),
        (wave_old_hbm, old.at[first]),
        (adj_old_hbm, old.at[second]),
        (source_hbm, driven.at[first]),
        (adj_source_hbm, driven.at[second]),
    ]
    loads = [
        pltpu.make_async_copy(source, target, load_sem.at[k])
        for k, (source, target) in enumerate(moves)
    ]
    for load in loads:
        load.start()
    barrier = pltpu.get_barrier_semaphore()
    for to_s, to_d, there in up + down:

        @pl.when(there)
        def _():
            pl.semaphore_signal(barrier, inc=1, device_id=(to_s, to_d), device_id_type=MESH)

    fill_tables(spread_ref, fold_ref)
    for load in loads[:2]:
        load.wait()
    for c in range(NODES_C):
        stage_a[c * 8 : c * 8 + 8, :] = fields[pl.ds(c, 8, stride=PLANE), :]
    for a in range(NODES_A):
        stage_c[a * 8 : a * 8 + 8, :] = fields[pl.ds(a * NODES_C, 8, stride=PLANE), :]
    peers = sum(there.astype(jnp.int32) for _, _, there in up + down)
    pl.semaphore_wait(barrier, peers)

    def remote(source, target, k, to):
        return pltpu.make_async_remote_copy(
            src_ref=source,
            dst_ref=target,
            send_sem=send_sem.at[k],
            recv_sem=recv_sem.at[k],
            device_id=(to[0], to[1]),
            device_id_type=MESH,
        )

    halos = [
        remote(stage_a, halo_a, 0, down[0]),
        remote(stage_c, halo_c, 1, down[1]),
        remote(stage_a.at[pl.ds(0, 8)], halo_d, 2, down[2]),
    ]
    for copy, (_, _, there) in zip(halos, down):

        @pl.when(there)
        def _():
            copy.start()

    for load in loads[2:9]:
        load.wait()
    rows = lax.broadcasted_iota(jnp.int32, (256, 256), 0)
    placing = jnp.where(cell_ref[0:1, :] == rows, 1.0, 0.0).astype(bf16)

    def to_cells(ref):
        high, low = two_terms(ref[...])
        return dot_rows(high, placing) + dot_rows(low, placing)

    scale = jnp.concatenate([scale_ref[0:125, :]] * 2, axis=1)
    density = to_cells(density_ref) * scale
    modulus = to_cells(modulus_ref) * scale
    pad = jnp.zeros((3, 256), f32)
    density = jnp.concatenate([density, pad], axis=0)
    modulus = jnp.concatenate([modulus, pad], axis=0)
    expand = ones_where(iota((1024, 128), 0) >> 3 == iota((1024, 128), 1))
    stiff[...] = dot_right(expand, density)
    mass_row, node_lane = iota((48, 128), 0), iota((48, 128), 1)
    select = jnp.concatenate(
        [
            ones_where(5 * (mass_row - 20 * ea) + r == node_lane)
            for r in range(5)
            for ea in range(2)
        ],
        axis=0,
    )
    picked = dot_right(select, modulus)
    for r in range(5):
        mass_lhs[:, r * 128 : (r + 1) * 128] = (
            picked[r * 96 : r * 96 + 48, 0:128] + picked[r * 96 + 48 : r * 96 + 96, 128:256]
        )
    mass_fold[...] = dot_left(mass_lhs[...], fold_ref[...])
    for a in range(NODES_A + 1):
        for ec in range(4):
            lanes = slice(ec * 128, ec * 128 + 128)
            mass_sum[a * 24 + 4 * ec : a * 24 + 4 * ec + 4, :] = mass_fold[a * 5 : a * 5 + 4, lanes]
        for ec in range(4):
            lanes = slice(ec * 128, ec * 128 + 128)
            tail = mass_fold[a * 5 + 4 : a * 5 + 5, lanes]
            row = a * 24 + 4 * ec + 4
            if ec < 3:
                mass_sum[row : row + 1, :] += tail
            else:
                mass_sum[row : row + 1, :] = tail

    slots = lax.broadcasted_iota(jnp.int32, (1, 256), 1)
    digit_rows = lax.broadcasted_iota(jnp.int32, (16, 256), 0)
    digits = jnp.zeros((16, 256), f32)
    for t in range(4):
        live = slots < count_ref[0:1, t : t + 1]
        number = jnp.where(live, brick_ref[t : t + 1, :] + 1, 0)
        pair = jnp.where(
            digit_rows == 2 * t,
            number >> 5,
            jnp.where(digit_rows == 2 * t + 1, number & 31, 0),
        )
        listed = jnp.where(elem_ref[t : t + 1, :] == rows, 1.0, 0.0).astype(bf16)
        digits = digits + dot_rows(pair.astype(f32).astype(bf16), listed)
    digits = dot_rows(digits.astype(bf16), placing)
    for ea in range(2):
        blocks_ref[0, ea, 128:144, :] = digits[:, ea * 128 : ea * 128 + 128]

    zeros = jnp.zeros((8, 128), f32)
    lhs[360:384, :] = jnp.zeros((24, 512), f32)

    def place(a, c, tile):
        ec, q = c // 4, c % 4
        if ec < 4:
            lhs[pl.ds(pl.multiple_of((a * 5 + q) * 8, 8), 8), ec * 128 : ec * 128 + 128] = tile
        if q == 0 and ec > 0:
            lhs[pl.ds(pl.multiple_of((a * 5 + 4) * 8, 8), 8), (ec - 1) * 128 : ec * 128] = tile

    def place_plane(a, carry):
        for c in range(NODES_C):
            place(a, c, fields[pl.ds(a * NODES_C + c, 8, stride=PLANE), :])
        return carry

    lax.fori_loop(0, NODES_A, place_plane, 0)

    for buffer, (_, _, there) in zip((halo_a, halo_c, halo_d), up):

        @pl.when(jnp.logical_not(there))
        def _():
            buffer[...] = jnp.zeros(buffer.shape, f32)

    for copy, (_, _, there) in zip(halos, down):

        @pl.when(there)
        def _():
            copy.wait_send()

    for copy, (_, _, there) in zip(halos, up):

        @pl.when(there)
        def _():
            copy.wait_recv()

    for c in range(NODES_C):
        place(8, c, halo_a[c * 8 : c * 8 + 8, :])
    for a in range(NODES_A):
        place(a, 16, halo_c[a * 8 : a * 8 + 8, :])
    place(8, 16, halo_d[...])

    def spread_rows(k, carry):
        at = pl.ds(pl.multiple_of(k * 128, 128), 128)
        values[at, :] = dot_left(lhs[at, :], spread_ref[...])
        return carry

    lax.fori_loop(0, 3, spread_rows, 0)
    product[1000:1024, :] = jnp.zeros((24, 256), f32)

    gather = ones_where(iota((128, 1024), 1) >> 3 == iota((128, 1024), 0), 0.5)

    def mates(g):
        return g * pltpu.roll(g, 4, 0)

    def eight(k):
        return pl.ds(pl.multiple_of(k * 8, 8), 8)

    def block_send(ea, k):
        own = 1 if k == 2 else 0
        return remote(
            blocks_ref.at[own, ea], blocks_ref.at[1 + k, ea], 3 + 3 * ea + k, up[1 if k else 0]
        )

    for k in range(3):

        @pl.when(jnp.logical_not(down[k][2]))
        def _():
            blocks_ref[1 + k] = jnp.zeros((2, BLOCK_ROWS, 128), f32)

    relayed = below_s & above_d

    def relay(ea):
        @pl.when(below_s)
        def _():
            block_send(ea, 0).wait_recv()

        @pl.when(relayed)
        def _():
            block_send(ea, 2).start()

    for ea in range(2):
        half = slice(ea * 128, ea * 128 + 128)

        def plane(p, carry):
            v = [
                [
                    values[eight((4 * ea + p) * 5 + q), r * 128 : r * 128 + 128]
                    for r in range(5)
                ]
                for q in range(5)
            ]
            k = [[stiff[eight(p * 25 + q * 5 + r), half] for r in range(5)] for q in range(5)]
            pair = [[None] * 5 for _ in range(5)]
            force = [[None] * 5 for _ in range(5)]
            for r in range(5):
                g = forward([v[q][r] for q in range(5)])
                f = backward([k[q][r] * g[q] for q in range(5)])
                for q in range(5):
                    pair[q][r] = mates(g[q])
                    force[q][r] = f[q]
            for q in range(5):
                g = forward(v[q])
                f = backward([k[q][r] * g[r] for r in range(5)])
                for r in range(5):
                    product[eight(p * 25 + q * 5 + r), half] = pair[q][r] + mates(g[r])
                    forces[eight(ea * 25 + p * 5 + q), r * 128 : r * 128 + 128] = force[q][r] + f[r]
            return carry

        lax.fori_loop(0, 5, plane, 0)

        def line(q, carry):
            for r in range(5):
                lanes = slice(r * 128, r * 128 + 128)
                g = forward([values[eight((4 * ea + p) * 5 + q), lanes] for p in range(5)])
                f = backward([stiff[eight(p * 25 + q * 5 + r), half] * g[p] for p in range(5)])
                for p in range(5):
                    product[eight(p * 25 + q * 5 + r), half] += mates(g[p])
                    forces[eight(ea * 25 + p * 5 + q), lanes] += f[p]
            return carry

        lax.fori_loop(0, 5, line, 0)

        blocks_ref[0, ea, 0:128, :] = dot_right(gather, product[:, half]) * (
            -time_step * scale_ref[...]
        )
        for k in range(2):

            @pl.when(up[k][2])
            def _():
                block_send(ea, k).start()

    forces[160:200, :] += forces[200:240, :]

    def fold_rows(first, count, at):
        folded[at : at + count, :] = dot_left(forces[first : first + count, :], fold_ref[...])

    fold_rows(0, 200, 0)
    fold_rows(240, 160, 200)

    def node(a, c):
        ec, q = c // 4, c % 4
        out = None
        if ec < 4:
            out = folded[eight(a * 5 + q), ec * 128 : ec * 128 + 128]
        if q == 0 and ec > 0:
            tail = folded[eight(a * 5 + 4), (ec - 1) * 128 : ec * 128]
            out = tail if out is None else out + tail
        return out

    for c in range(NODES_C):
        face_a[c * 8 : c * 8 + 8, :] = node(8, c)
    face_a[128:144, :] = mass_sum[192:208, :]
    for a in range(NODES_A):
        face_c[a * 8 : a * 8 + 8, :] = node(a, 16)
        face_c[64 + a : 65 + a, :] = mass_sum[a * 24 + 16 : a * 24 + 17, :]
    face_d[0:8, :] = node(8, 16)
    face_d[8:16, :] = jnp.broadcast_to(mass_sum[208:209, :], (8, 128))
    faces = [
        remote(face_a, got_a, 9, up[0]),
        remote(face_c, got_c, 10, up[1]),
        remote(face_d, got_d, 11, up[2]),
    ]
    for copy, (_, _, there) in zip(faces, up):

        @pl.when(there)
        def _():
            copy.start()

    for buffer, (_, _, there) in zip((got_a, got_c, got_d), down):

        @pl.when(jnp.logical_not(there))
        def _():
            buffer[...] = jnp.zeros(buffer.shape, f32)

    relay(0)

    def into_bricks(t):
        block = jnp.concatenate([blocks_ref[t, 0], blocks_ref[t, 1]], axis=1)
        stacked = jnp.concatenate(two_terms(block[0:128]), axis=0)
        row = 128 + 2 * t
        target = block[row : row + 1] * 32.0 + block[row + 1 : row + 2] - 1.0
        for n in range(bricks.shape[1] // 256):
            part = dot_rows(stacked, ones_where(target == (rows + n * 256).astype(f32)))
            part = part[0:125] + part[128:253]
            lanes = slice(n * 256, n * 256 + 256)
            if t == 0:
                bricks[:, lanes] = part
            else:
                bricks[:, lanes] += part

    def write_plane(a, carry):
        for c in range(1, NODES_C):
            next_ref[pl.ds(a * NODES_C + c, 8, stride=PLANE), :] = node(a, c)
        return carry

    lax.fori_loop(1, NODES_A, write_plane, 0)
    into_bricks(0)
    for load in loads[9:]:
        load.wait()
    relay(1)

    for copy, (_, _, there) in zip(faces, up):

        @pl.when(there)
        def _():
            copy.wait_send()

    for copy, (_, _, there) in zip(faces, down):

        @pl.when(there)
        def _():
            copy.wait_recv()

    for c in range(1, NODES_C):
        next_ref[pl.ds(c, 8, stride=PLANE), :] = node(0, c) + got_a[c * 8 : c * 8 + 8, :]
    for a in range(1, NODES_A):
        next_ref[pl.ds(a * NODES_C, 8, stride=PLANE), :] = (
            node(a, 0) + got_c[a * 8 : a * 8 + 8, :]
        )
    next_ref[pl.ds(0, 8, stride=PLANE), :] = (
        node(0, 0) + got_a[0:8, :] + got_c[0:8, :] + got_d[0:8, :]
    )
    mass_sum[0:16, :] += got_a[128:144, :]
    for a in range(NODES_A):
        mass_sum[a * 24 : a * 24 + 1, :] += got_c[64 + a : 65 + a, :]
    mass_sum[0:1, :] += got_d[8:9, :]
    inverse = jnp.concatenate([mass_sum[a * 24 : a * 24 + 16, :] for a in range(NODES_A)], axis=0)
    inverse = time_step * time_step / inverse

    def update(x, carry):
        at = pl.ds(pl.multiple_of(x * PLANE, PLANE), PLANE)
        next_ref[at, :] = (
            2.0 * fields[at, :] - old[at, :] + (driven[at, :] - next_ref[at, :]) * inverse
        )
        return carry

    lax.fori_loop(0, 8, update, 0)

    writes = [
        pltpu.make_async_copy(next_ref.at[first], wave_out, write_sem.at[0]),
        pltpu.make_async_copy(next_ref.at[second], adj_out, write_sem.at[1]),
        pltpu.make_async_copy(bricks, brick_out, write_sem.at[2]),
    ]
    for write in writes[:2]:
        write.start()
    into_bricks(1)
    for k in (1, 2):
        for ea in range(2):

            @pl.when(down[k][2])
            def _():
                block_send(ea, k).wait_recv()

        into_bricks(1 + k)
    writes[2].start()
    for ea in range(2):
        for k, sent in enumerate((above_s, above_d, relayed)):

            @pl.when(sent)
            def _():
                block_send(ea, k).wait_send()

    for write in writes:
        write.wait()


def hand_over(*refs):
    sources, targets, sem = refs[:3], refs[3:6], refs[6]
    copies = [
        pltpu.make_async_copy(source, target, sem.at[k])
        for k, (source, target) in enumerate(zip(sources, targets))
    ]
    for copy in copies:
        copy.start()
    for copy in copies:
        copy.wait()


def per_device(
    n_surf,
    n_depth,
    wave_now,
    wave_old,
    adj_now,
    adj_old,
    source,
    adj_source,
    inv_density,
    inv_modulus,
    element_cell,
    send_elem,
    send_brick,
    send_count,
):
    scale = cubature_rows()
    anywhere = pl.BlockSpec(memory_space=pl.ANY)

    def flat(x):
        return x.reshape(4 * PLANE, 128)

    operands = [
        flat(wave_now),
        flat(adj_now),
        element_cell,
        send_elem[0],
        send_brick[0],
        send_count,
        inv_density,
        inv_modulus,
        jnp.asarray(scale, f32),
        flat(wave_old),
        flat(adj_old),
        flat(source),
        flat(adj_source),
    ]
    held = [pltpu.VMEM(x.shape, x.dtype) for x in operands[2:9]]
    half = jax.ShapeDtypeStruct((4 * PLANE, 128), f32)
    results = (half, half, jax.ShapeDtypeStruct((125, 1024), f32))
    results_here = pl.pallas_call(
        functools.partial(body, n_surf, n_depth),
        out_shape=results,
        in_specs=[anywhere] * len(operands),
        out_specs=(anywhere,) * 3,
        scratch_shapes=[
            pltpu.VMEM((8 * PLANE, 128), f32),
            pltpu.VMEM((4, 2, BLOCK_ROWS, 128), f32),
            pltpu.VMEM((125, 1024), f32),
            pltpu.VMEM((8 * PLANE, 128), f32),
        ]
        + held
        + [
            pltpu.VMEM((640, 512), bf16),
            pltpu.VMEM((512, 640), bf16),
            pltpu.VMEM((8 * PLANE, 128), f32),
            pltpu.VMEM((8 * PLANE, 128), f32),
            pltpu.VMEM((128, 128), f32),
            pltpu.VMEM((64, 128), f32),
            pltpu.VMEM((8, 128), f32),
            pltpu.VMEM((128, 128), f32),
            pltpu.VMEM((64, 128), f32),
            pltpu.VMEM((384, 512), f32),
            pltpu.VMEM((384, 640), f32),
            pltpu.VMEM((1024, 256), f32),
            pltpu.VMEM((1024, 256), f32),
            pltpu.VMEM((400, 640), f32),
            pltpu.VMEM((360, 512), f32),
            pltpu.VMEM((48, 640), f32),
            pltpu.VMEM((48, 512), f32),
            pltpu.VMEM((216, 128), f32),
            pltpu.VMEM((FACE_A, 128), f32),
            pltpu.VMEM((FACE_C, 128), f32),
            pltpu.VMEM((FACE_D, 128), f32),
            pltpu.VMEM((FACE_A, 128), f32),
            pltpu.VMEM((FACE_C, 128), f32),
            pltpu.VMEM((FACE_D, 128), f32),
            pltpu.SemaphoreType.DMA((3,)),
            pltpu.SemaphoreType.DMA((len(operands),)),
            pltpu.SemaphoreType.DMA((12,)),
            pltpu.SemaphoreType.DMA((12,)),
        ],
        compiler_params=pltpu.CompilerParams(
            collective_id=0, has_side_effects=True, vmem_limit_bytes=60 * 1024 * 1024
        ),
    )(*operands)
    wave_next, adj_next, brick_kernel = pl.pallas_call(
        hand_over,
        out_shape=results,
        in_specs=[anywhere] * 3,
        out_specs=(anywhere,) * 3,
        scratch_shapes=[pltpu.SemaphoreType.DMA((3,))],
        compiler_params=pltpu.CompilerParams(vmem_limit_bytes=60 * 1024 * 1024),
    )(*results_here)
    shape = wave_now.shape
    return wave_next.reshape(shape), adj_next.reshape(shape), brick_kernel


def solution(mesh):
    field = P(None, "surf", "depth", None)
    column = P(None, ("surf", "depth"))
    placed = (field,) * 6 + (
        column,
        column,
        P(("surf", "depth"), None),
        P(("surf", "depth"), None, None),
        P(("surf", "depth"), None, None),
        P(("surf", "depth"), None),
    )
    return jax.shard_map(
        functools.partial(per_device, mesh.shape["surf"], mesh.shape["depth"]),
        mesh=mesh,
        in_specs=placed,
        out_specs=(field, field, column),
        check_vma=False,
    )
```

```python
import functools
import math

import jax
import jax.numpy as jnp
import numpy as np
from jax import lax
from jax.experimental import pallas as pl
from jax.experimental.pallas import tpu as pltpu
from jax.sharding import PartitionSpec as P

time_step = 0.05
MESH = pl.DeviceIdType.MESH
f32 = jnp.float32
bf16 = jnp.bfloat16

NODES_A, NODES_C, NODES_B = 8, 16, 128
PLANE = NODES_A * NODES_C
BLOCK_ROWS = 144
FACE_A, FACE_C, FACE_D = 144, 72, 16


def gll_numbers():
    points = np.array([-1.0, -math.sqrt(3.0 / 7.0), 0.0, math.sqrt(3.0 / 7.0), 1.0])
    weights = np.array([0.1, 49.0 / 90.0, 32.0 / 45.0, 49.0 / 90.0, 0.1])
    identity = np.eye(5)
    on_diagonal = identity > 0.5
    differences = points[:, None] - points[None, :] + identity
    products = np.prod(differences, axis=1)
    derivative = products[:, None] / products[None, :] / differences
    inverse = np.where(on_diagonal, 0.0, 1.0 / differences)
    derivative = np.where(on_diagonal, inverse.sum(axis=1)[:, None], derivative)
    return derivative, weights


D, W = gll_numbers()


def cubature_rows():
    cubature = (W[:, None, None] * W[None, :, None] * W[None, None, :]).reshape(-1)
    scale = np.zeros((128, 128), np.float32)
    scale[:125] = cubature[:, None]
    return scale


def iota(shape, axis):
    return lax.broadcasted_iota(jnp.int32, shape, axis)


def ones_where(condition, one=1.0):
    return jnp.where(condition, one, 0.0).astype(bf16)


def fill_tables(spread_ref, fold_ref):
    row, lane = iota((128, 128), 0), iota((128, 128), 1)
    lane_one, row_one = iota((1, 128), 1), iota((128, 1), 0)
    for ec in range(4):
        for r in range(5):
            node = jnp.where(lane_one >> 5 == ec, (4 * (lane_one & 31) + r) & 127, -1)
            spread_ref[ec * 128 : ec * 128 + 128, r * 128 : r * 128 + 128] = ones_where(row == node)
            node = jnp.where(row_one >> 5 == ec, (4 * (row_one & 31) + r) & 127, -1)
            fold_ref[r * 128 : r * 128 + 128, ec * 128 : ec * 128 + 128] = ones_where(lane == node)


def two_terms(x):
    high = x.astype(bf16)
    return high, (x - high.astype(f32)).astype(bf16)


def dot_left(x, table):
    both = jnp.dot(jnp.concatenate(two_terms(x), axis=0), table, preferred_element_type=f32)
    return both[: x.shape[0]] + both[x.shape[0] :]


def dot_right(table, x):
    high, low = two_terms(x)
    return jnp.dot(table, high, preferred_element_type=f32) + jnp.dot(
        table, low, preferred_element_type=f32
    )


def dot_rows(x, table):
    return lax.dot_general(x, table, (((1,), (1,)), ((), ())), preferred_element_type=f32)


def forward(v):
    s0, s1, d0, d1 = v[0] + v[4], v[1] + v[3], v[0] - v[4], v[1] - v[3]
    out = [None] * 5
    for i in range(2):
        even = (
            float((D[i, 0] + D[i, 4]) / 2) * s0
            + float((D[i, 1] + D[i, 3]) / 2) * s1
            + float(D[i, 2]) * v[2]
        )
        odd = float((D[i, 0] - D[i, 4]) / 2) * d0 + float((D[i, 1] - D[i, 3]) / 2) * d1
        out[i] = even + odd
        out[4 - i] = odd - even
    out[2] = float(D[2, 0]) * d0 + float(D[2, 1]) * d1
    return out


def backward(h):
    s0, s1, d0, d1 = h[0] + h[4], h[1] + h[3], h[0] - h[4], h[1] - h[3]
    out = [None] * 5
    for p in range(2):
        even = (
            float((D[0, p] + D[4, p]) / 2) * s0
            + float((D[1, p] + D[3, p]) / 2) * s1
            + float(D[2, p]) * h[2]
        )
        odd = float((D[0, p] - D[4, p]) / 2) * d0 + float((D[1, p] - D[3, p]) / 2) * d1
        out[p] = even + odd
        out[4 - p] = odd - even
    out[2] = float(D[0, 2]) * d0 + float(D[1, 2]) * d1
    return out


def body(
    n_surf,
    n_depth,
    wave_hbm,
    adj_hbm,
    cell_hbm,
    elem_hbm,
    brick_hbm,
    count_hbm,
    density_hbm,
    modulus_hbm,
    scale_hbm,
    wave_old_hbm,
    adj_old_hbm,
    source_hbm,
    adj_source_hbm,
    wave_out,
    adj_out,
    brick_out,
    next_ref,
    blocks_ref,
    bricks,
    fields,
    cell_ref,
    elem_ref,
    brick_ref,
    count_ref,
    density_ref,
    modulus_ref,
    scale_ref,
    fold_ref,
    spread_ref,
    old,
    driven,
    halo_a,
    halo_c,
    halo_d,
    stage_a,
    stage_c,
    lhs,
    values,
    stiff,
    product,
    forces,
    folded,
    mass_lhs,
    mass_fold,
    mass_sum,
    face_a,
    face_c,
    face_d,
    got_a,
    got_c,
    got_d,
    write_sem,
    load_sem,
    send_sem,
    recv_sem,
):
    s = lax.axis_index("surf")
    d = lax.axis_index("depth")
    above_s, above_d = s < n_surf - 1, d < n_depth - 1
    below_s, below_d = s > 0, d > 0
    above_both, below_both = above_s & above_d, below_s & below_d
    up = ((s + 1, d, above_s), (s, d + 1, above_d), (s + 1, d + 1, above_both))
    down = ((s - 1, d, below_s), (s, d - 1, below_d), (s - 1, d - 1, below_both))

    first, second = pl.ds(0, 4 * PLANE), pl.ds(4 * PLANE, 4 * PLANE)
    moves = [
        (wave_hbm, fields.at[first]),
        (adj_hbm, fields.at[second]),
        (cell_hbm, cell_ref),
        (density_hbm, density_ref),
        (modulus_hbm, modulus_ref),
        (scale_hbm, scale_ref),
        (elem_hbm, elem_ref),
        (brick_hbm, brick_ref),
        (count_hbm, count_ref),
        (wave_old_hbm, old.at[first]),
        (adj_old_hbm, old.at[second]),
        (source_hbm, driven.at[first]),
        (adj_source_hbm, driven.at[second]),
    ]
    loads = [
        pltpu.make_async_copy(source, target, load_sem.at[k])
        for k, (source, target) in enumerate(moves)
    ]
    for load in loads:
        load.start()
    barrier = pltpu.get_barrier_semaphore()
    for to_s, to_d, there in up + down:

        @pl.when(there)
        def _():
            pl.semaphore_signal(barrier, inc=1, device_id=(to_s, to_d), device_id_type=MESH)

    fill_tables(spread_ref, fold_ref)
    for load in loads[:2]:
        load.wait()
    for c in range(NODES_C):
        stage_a[c * 8 : c * 8 + 8, :] = fields[pl.ds(c, 8, stride=PLANE), :]
    for a in range(NODES_A):
        stage_c[a * 8 : a * 8 + 8, :] = fields[pl.ds(a * NODES_C, 8, stride=PLANE), :]
    peers = sum(there.astype(jnp.int32) for _, _, there in up + down)
    pl.semaphore_wait(barrier, peers)

    def remote(source, target, k, to):
        return pltpu.make_async_remote_copy(
            src_ref=source,
            dst_ref=target,
            send_sem=send_sem.at[k],
            recv_sem=recv_sem.at[k],
            device_id=(to[0], to[1]),
            device_id_type=MESH,
        )

    halos = [
        remote(stage_a, halo_a, 0, down[0]),
        remote(stage_c, halo_c, 1, down[1]),
        remote(stage_a.at[pl.ds(0, 8)], halo_d, 2, down[2]),
    ]
    for copy, (_, _, there) in zip(halos, down):

        @pl.when(there)
        def _():
            copy.start()

    for load in loads[2:9]:
        load.wait()
    rows = lax.broadcasted_iota(jnp.int32, (256, 256), 0)
    placing = jnp.where(cell_ref[0:1, :] == rows, 1.0, 0.0).astype(bf16)

    def to_cells(ref):
        high, low = two_terms(ref[...])
        return dot_rows(high, placing) + dot_rows(low, placing)

    scale = jnp.concatenate([scale_ref[0:125, :]] * 2, axis=1)
    density = to_cells(density_ref) * scale
    modulus = to_cells(modulus_ref) * scale
    pad = jnp.zeros((3, 256), f32)
    density = jnp.concatenate([density, pad], axis=0)
    modulus = jnp.concatenate([modulus, pad], axis=0)
    expand = ones_where(iota((1024, 128), 0) >> 3 == iota((1024, 128), 1))
    stiff[...] = dot_right(expand, density)
    mass_row, node_lane = iota((48, 128), 0), iota((48, 128), 1)
    select = jnp.concatenate(
        [
            ones_where(5 * (mass_row - 20 * ea) + r == node_lane)
            for r in range(5)
            for ea in range(2)
        ],
        axis=0,
    )
    picked = dot_right(select, modulus)
    for r in range(5):
        mass_lhs[:, r * 128 : (r + 1) * 128] = (
            picked[r * 96 : r * 96 + 48, 0:128] + picked[r * 96 + 48 : r * 96 + 96, 128:256]
        )
    mass_fold[...] = dot_left(mass_lhs[...], fold_ref[...])
    for a in range(NODES_A + 1):
        for ec in range(4):
            lanes = slice(ec * 128, ec * 128 + 128)
            mass_sum[a * 24 + 4 * ec : a * 24 + 4 * ec + 4, :] = mass_fold[a * 5 : a * 5 + 4, lanes]
        for ec in range(4):
            lanes = slice(ec * 128, ec * 128 + 128)
            tail = mass_fold[a * 5 + 4 : a * 5 + 5, lanes]
            row = a * 24 + 4 * ec + 4
            if ec < 3:
                mass_sum[row : row + 1, :] += tail
            else:
                mass_sum[row : row + 1, :] = tail

    slots = lax.broadcasted_iota(jnp.int32, (1, 256), 1)
    digit_rows = lax.broadcasted_iota(jnp.int32, (16, 256), 0)
    digits = jnp.zeros((16, 256), f32)
    for t in range(4):
        live = slots < count_ref[0:1, t : t + 1]
        number = jnp.where(live, brick_ref[t : t + 1, :] + 1, 0)
        pair = jnp.where(
            digit_rows == 2 * t,
            number >> 5,
            jnp.where(digit_rows == 2 * t + 1, number & 31, 0),
        )
        listed = jnp.where(elem_ref[t : t + 1, :] == rows, 1.0, 0.0).astype(bf16)
        digits = digits + dot_rows(pair.astype(f32).astype(bf16), listed)
    digits = dot_rows(digits.astype(bf16), placing)
    for ea in range(2):
        blocks_ref[0, ea, 128:144, :] = digits[:, ea * 128 : ea * 128 + 128]

    zeros = jnp.zeros((8, 128), f32)
    lhs[360:384, :] = jnp.zeros((24, 512), f32)
    forces[200:384, :] = jnp.zeros((184, 640), f32)

    def place(a, c, tile):
        ec, q = c // 4, c % 4
        if ec < 4:
            lhs[pl.ds(pl.multiple_of((a * 5 + q) * 8, 8), 8), ec * 128 : ec * 128 + 128] = tile
        if q == 0 and ec > 0:
            lhs[pl.ds(pl.multiple_of((a * 5 + 4) * 8, 8), 8), (ec - 1) * 128 : ec * 128] = tile

    def place_plane(a, carry):
        for c in range(NODES_C):
            place(a, c, fields[pl.ds(a * NODES_C + c, 8, stride=PLANE), :])
        return carry

    lax.fori_loop(0, NODES_A, place_plane, 0)

    for buffer, (_, _, there) in zip((halo_a, halo_c, halo_d), up):

        @pl.when(jnp.logical_not(there))
        def _():
            buffer[...] = jnp.zeros(buffer.shape, f32)

    for copy, (_, _, there) in zip(halos, down):

        @pl.when(there)
        def _():
            copy.wait_send()

    for copy, (_, _, there) in zip(halos, up):

        @pl.when(there)
        def _():
            copy.wait_recv()

    for c in range(NODES_C):
        place(8, c, halo_a[c * 8 : c * 8 + 8, :])
    for a in range(NODES_A):
        place(a, 16, halo_c[a * 8 : a * 8 + 8, :])
    place(8, 16, halo_d[...])

    values[...] = dot_left(lhs[...], spread_ref[...])
    product[1000:1024, :] = jnp.zeros((24, 256), f32)

    gather = ones_where(iota((128, 1024), 1) >> 3 == iota((128, 1024), 0), 0.5)

    def mates(g):
        return g * pltpu.roll(g, 4, 0)

    def eight(k):
        return pl.ds(pl.multiple_of(k * 8, 8), 8)

    def block_send(ea, k):
        own = 1 if k == 2 else 0
        return remote(
            blocks_ref.at[own, ea], blocks_ref.at[1 + k, ea], 3 + 3 * ea + k, up[1 if k else 0]
        )

    for k in range(3):

        @pl.when(jnp.logical_not(down[k][2]))
        def _():
            blocks_ref[1 + k] = jnp.zeros((2, BLOCK_ROWS, 128), f32)

    relayed = below_s & above_d

    def relay(ea):
        @pl.when(below_s)
        def _():
            block_send(ea, 0).wait_recv()

        @pl.when(relayed)
        def _():
            block_send(ea, 2).start()

    for ea in range(2):
        half = slice(ea * 128, ea * 128 + 128)

        def plane(p, carry):
            v = [
                [
                    values[eight((4 * ea + p) * 5 + q), r * 128 : r * 128 + 128]
                    for r in range(5)
                ]
                for q in range(5)
            ]
            k = [[stiff[eight(p * 25 + q * 5 + r), half] for r in range(5)] for q in range(5)]
            pair = [[None] * 5 for _ in range(5)]
            force = [[None] * 5 for _ in range(5)]
            for r in range(5):
                g = forward([v[q][r] for q in range(5)])
                f = backward([k[q][r] * g[q] for q in range(5)])
                for q in range(5):
                    pair[q][r] = mates(g[q])
                    force[q][r] = f[q]
            for q in range(5):
                g = forward(v[q])
                f = backward([k[q][r] * g[r] for r in range(5)])
                for r in range(5):
                    product[eight(p * 25 + q * 5 + r), half] = pair[q][r] + mates(g[r])
                    at = eight((4 * ea + p) * 5 + q), slice(r * 128, r * 128 + 128)
                    total = force[q][r] + f[r]
                    forces[at] = total if ea == 0 else forces[at] + total
            return carry

        lax.fori_loop(0, 5, plane, 0)

        def line(q, carry):
            for r in range(5):
                lanes = slice(r * 128, r * 128 + 128)
                g = forward([values[eight((4 * ea + p) * 5 + q), lanes] for p in range(5)])
                f = backward([stiff[eight(p * 25 + q * 5 + r), half] * g[p] for p in range(5)])
                for p in range(5):
                    product[eight(p * 25 + q * 5 + r), half] += mates(g[p])
                    forces[eight((4 * ea + p) * 5 + q), lanes] += f[p]
            return carry

        lax.fori_loop(0, 5, line, 0)

        blocks_ref[0, ea, 0:128, :] = dot_right(gather, product[:, half]) * (
            -time_step * scale_ref[...]
        )
        for k in range(2):

            @pl.when(up[k][2])
            def _():
                block_send(ea, k).start()

    folded[...] = dot_left(forces[...], fold_ref[...])

    def node(a, c):
        ec, q = c // 4, c % 4
        out = None
        if ec < 4:
            out = folded[eight(a * 5 + q), ec * 128 : ec * 128 + 128]
        if q == 0 and ec > 0:
            tail = folded[eight(a * 5 + 4), (ec - 1) * 128 : ec * 128]
            out = tail if out is None else out + tail
        return out

    for c in range(NODES_C):
        face_a[c * 8 : c * 8 + 8, :] = node(8, c)
    face_a[128:144, :] = mass_sum[192:208, :]
    for a in range(NODES_A):
        face_c[a * 8 : a * 8 + 8, :] = node(a, 16)
        face_c[64 + a : 65 + a, :] = mass_sum[a * 24 + 16 : a * 24 + 17, :]
    face_d[0:8, :] = node(8, 16)
    face_d[8:16, :] = jnp.broadcast_to(mass_sum[208:209, :], (8, 128))
    faces = [
        remote(face_a, got_a, 9, up[0]),
        remote(face_c, got_c, 10, up[1]),
        remote(face_d, got_d, 11, up[2]),
    ]
    for copy, (_, _, there) in zip(faces, up):

        @pl.when(there)
        def _():
            copy.start()

    for buffer, (_, _, there) in zip((got_a, got_c, got_d), down):

        @pl.when(jnp.logical_not(there))
        def _():
            buffer[...] = jnp.zeros(buffer.shape, f32)

    relay(0)

    def arrived(k):
        for ea in range(2):

            @pl.when(down[k][2])
            def _():
                block_send(ea, k).wait_recv()

    def into_bricks(t):
        block = jnp.concatenate([blocks_ref[t, 0], blocks_ref[t, 1]], axis=1)
        stacked = jnp.concatenate(two_terms(block[0:128]), axis=0)
        row = 128 + 2 * t
        target = block[row : row + 1] * 32.0 + block[row + 1 : row + 2] - 1.0
        for n in range(bricks.shape[1] // 256):
            part = dot_rows(stacked, ones_where(target == (rows + n * 256).astype(f32)))
            part = part[0:125] + part[128:253]
            lanes = slice(n * 256, n * 256 + 256)
            if t == 0:
                bricks[:, lanes] = part
            else:
                bricks[:, lanes] += part

    def write_plane(a, carry):
        for c in range(1, NODES_C):
            next_ref[pl.ds(a * NODES_C + c, 8, stride=PLANE), :] = node(a, c)
        return carry

    lax.fori_loop(1, NODES_A, write_plane, 0)
    into_bricks(0)
    for load in loads[9:]:
        load.wait()
    relay(1)
    into_bricks(1)
    arrived(1)
    into_bricks(2)

    for copy, (_, _, there) in zip(faces, up):

        @pl.when(there)
        def _():
            copy.wait_send()

    for copy, (_, _, there) in zip(faces, down):

        @pl.when(there)
        def _():
            copy.wait_recv()

    for c in range(1, NODES_C):
        next_ref[pl.ds(c, 8, stride=PLANE), :] = node(0, c) + got_a[c * 8 : c * 8 + 8, :]
    for a in range(1, NODES_A):
        next_ref[pl.ds(a * NODES_C, 8, stride=PLANE), :] = (
            node(a, 0) + got_c[a * 8 : a * 8 + 8, :]
        )
    next_ref[pl.ds(0, 8, stride=PLANE), :] = (
        node(0, 0) + got_a[0:8, :] + got_c[0:8, :] + got_d[0:8, :]
    )
    mass_sum[0:16, :] += got_a[128:144, :]
    for a in range(NODES_A):
        mass_sum[a * 24 : a * 24 + 1, :] += got_c[64 + a : 65 + a, :]
    mass_sum[0:1, :] += got_d[8:9, :]
    inverse = jnp.concatenate([mass_sum[a * 24 : a * 24 + 16, :] for a in range(NODES_A)], axis=0)
    inverse = time_step * time_step / inverse

    def update(x, carry):
        at = pl.ds(pl.multiple_of(x * PLANE, PLANE), PLANE)
        next_ref[at, :] = (
            2.0 * fields[at, :] - old[at, :] + (driven[at, :] - next_ref[at, :]) * inverse
        )
        return carry

    lax.fori_loop(0, 8, update, 0)

    writes = [
        pltpu.make_async_copy(next_ref.at[first], wave_out, write_sem.at[0]),
        pltpu.make_async_copy(next_ref.at[second], adj_out, write_sem.at[1]),
        pltpu.make_async_copy(bricks, brick_out, write_sem.at[2]),
    ]
    for write in writes[:2]:
        write.start()
    arrived(2)
    into_bricks(3)
    writes[2].start()
    for ea in range(2):
        for k, sent in enumerate((above_s, above_d, relayed)):

            @pl.when(sent)
            def _():
                block_send(ea, k).wait_send()

    for write in writes:
        write.wait()


def hand_over(*refs):
    sources, targets, held, sem = refs[:3], refs[3:6], refs[6:9], refs[9]
    loads = [
        pltpu.make_async_copy(source, mine, sem.at[k])
        for k, (source, mine) in enumerate(zip(sources, held))
    ]
    stores = [
        pltpu.make_async_copy(mine, target, sem.at[3 + k])
        for k, (mine, target) in enumerate(zip(held, targets))
    ]
    for load in loads:
        load.start()
    for load, store in zip(loads, stores):
        load.wait()
        store.start()
    for store in stores:
        store.wait()


def per_device(
    n_surf,
    n_depth,
    wave_now,
    wave_old,
    adj_now,
    adj_old,
    source,
    adj_source,
    inv_density,
    inv_modulus,
    element_cell,
    send_elem,
    send_brick,
    send_count,
):
    scale = cubature_rows()
    anywhere = pl.BlockSpec(memory_space=pl.ANY)

    def flat(x):
        return x.reshape(4 * PLANE, 128)

    operands = [
        flat(wave_now),
        flat(adj_now),
        element_cell,
        send_elem[0],
        send_brick[0],
        send_count,
        inv_density,
        inv_modulus,
        jnp.asarray(scale, f32),
        flat(wave_old),
        flat(adj_old),
        flat(source),
        flat(adj_source),
    ]
    held = [pltpu.VMEM(x.shape, x.dtype) for x in operands[2:9]]
    half = jax.ShapeDtypeStruct((4 * PLANE, 128), f32)
    results = (half, half, jax.ShapeDtypeStruct((125, 1024), f32))
    results_here = pl.pallas_call(
        functools.partial(body, n_surf, n_depth),
        out_shape=results,
        in_specs=[anywhere] * len(operands),
        out_specs=(anywhere,) * 3,
        scratch_shapes=[
            pltpu.VMEM((8 * PLANE, 128), f32),
            pltpu.VMEM((4, 2, BLOCK_ROWS, 128), f32),
            pltpu.VMEM((125, 1024), f32),
            pltpu.VMEM((8 * PLANE, 128), f32),
        ]
        + held
        + [
            pltpu.VMEM((640, 512), bf16),
            pltpu.VMEM((512, 640), bf16),
            pltpu.VMEM((8 * PLANE, 128), f32),
            pltpu.VMEM((8 * PLANE, 128), f32),
            pltpu.VMEM((128, 128), f32),
            pltpu.VMEM((64, 128), f32),
            pltpu.VMEM((8, 128), f32),
            pltpu.VMEM((128, 128), f32),
            pltpu.VMEM((64, 128), f32),
            pltpu.VMEM((384, 512), f32),
            pltpu.VMEM((384, 640), f32),
            pltpu.VMEM((1024, 256), f32),
            pltpu.VMEM((1024, 256), f32),
            pltpu.VMEM((384, 640), f32),
            pltpu.VMEM((384, 512), f32),
            pltpu.VMEM((48, 640), f32),
            pltpu.VMEM((48, 512), f32),
            pltpu.VMEM((216, 128), f32),
            pltpu.VMEM((FACE_A, 128), f32),
            pltpu.VMEM((FACE_C, 128), f32),
            pltpu.VMEM((FACE_D, 128), f32),
            pltpu.VMEM((FACE_A, 128), f32),
            pltpu.VMEM((FACE_C, 128), f32),
            pltpu.VMEM((FACE_D, 128), f32),
            pltpu.SemaphoreType.DMA((3,)),
            pltpu.SemaphoreType.DMA((len(operands),)),
            pltpu.SemaphoreType.DMA((12,)),
            pltpu.SemaphoreType.DMA((12,)),
        ],
        compiler_params=pltpu.CompilerParams(
            collective_id=0, has_side_effects=True, vmem_limit_bytes=60 * 1024 * 1024
        ),
    )(*operands)
    wave_next, adj_next, brick_kernel = pl.pallas_call(
        hand_over,
        out_shape=results,
        in_specs=[anywhere] * 3,
        out_specs=(anywhere,) * 3,
        scratch_shapes=[pltpu.VMEM(x.shape, f32) for x in results]
        + [pltpu.SemaphoreType.DMA((6,))],
        compiler_params=pltpu.CompilerParams(vmem_limit_bytes=60 * 1024 * 1024),
    )(*results_here)
    shape = wave_now.shape
    return wave_next.reshape(shape), adj_next.reshape(shape), brick_kernel


def solution(mesh):
    field = P(None, "surf", "depth", None)
    column = P(None, ("surf", "depth"))
    placed = (field,) * 6 + (
        column,
        column,
        P(("surf", "depth"), None),
        P(("surf", "depth"), None, None),
        P(("surf", "depth"), None, None),
        P(("surf", "depth"), None),
    )
    return jax.shard_map(
        functools.partial(per_device, mesh.shape["surf"], mesh.shape["depth"]),
        mesh=mesh,
        in_specs=placed,
        out_specs=(field, field, column),
        check_vma=False,
    )
```

```python
import functools
import math

import jax
import jax.numpy as jnp
import numpy as np
from jax import lax
from jax.experimental import pallas as pl
from jax.experimental.pallas import tpu as pltpu
from jax.sharding import PartitionSpec as P

time_step = 0.05
MESH = pl.DeviceIdType.MESH
f32 = jnp.float32
bf16 = jnp.bfloat16

NODES_A, NODES_C, NODES_B = 8, 16, 128
PLANE = NODES_A * NODES_C
BLOCK_ROWS = 144
FACE_A, FACE_C, FACE_D = 144, 72, 16


def gll_numbers():
    points = np.array([-1.0, -math.sqrt(3.0 / 7.0), 0.0, math.sqrt(3.0 / 7.0), 1.0])
    weights = np.array([0.1, 49.0 / 90.0, 32.0 / 45.0, 49.0 / 90.0, 0.1])
    identity = np.eye(5)
    on_diagonal = identity > 0.5
    differences = points[:, None] - points[None, :] + identity
    products = np.prod(differences, axis=1)
    derivative = products[:, None] / products[None, :] / differences
    inverse = np.where(on_diagonal, 0.0, 1.0 / differences)
    derivative = np.where(on_diagonal, inverse.sum(axis=1)[:, None], derivative)
    return derivative, weights


D, W = gll_numbers()


def cubature_rows():
    cubature = (W[:, None, None] * W[None, :, None] * W[None, None, :]).reshape(-1)
    scale = np.zeros((128, 128), np.float32)
    scale[:125] = cubature[:, None]
    return scale


def iota(shape, axis):
    return lax.broadcasted_iota(jnp.int32, shape, axis)


def ones_where(condition, one=1.0):
    return jnp.where(condition, one, 0.0).astype(bf16)


def fill_tables(spread_ref, fold_ref):
    row, lane = iota((128, 128), 0), iota((128, 128), 1)
    lane_one, row_one = iota((1, 128), 1), iota((128, 1), 0)
    for ec in range(4):
        for r in range(5):
            node = jnp.where(lane_one >> 5 == ec, (4 * (lane_one & 31) + r) & 127, -1)
            spread_ref[ec * 128 : ec * 128 + 128, r * 128 : r * 128 + 128] = ones_where(row == node)
            node = jnp.where(row_one >> 5 == ec, (4 * (row_one & 31) + r) & 127, -1)
            fold_ref[r * 128 : r * 128 + 128, ec * 128 : ec * 128 + 128] = ones_where(lane == node)


def two_terms(x):
    high = x.astype(bf16)
    return high, (x - high.astype(f32)).astype(bf16)


def dot_left(x, table):
    both = jnp.dot(jnp.concatenate(two_terms(x), axis=0), table, preferred_element_type=f32)
    return both[: x.shape[0]] + both[x.shape[0] :]


def dot_right(table, x):
    high, low = two_terms(x)
    return jnp.dot(table, high, preferred_element_type=f32) + jnp.dot(
        table, low, preferred_element_type=f32
    )


def dot_rows(x, table):
    return lax.dot_general(x, table, (((1,), (1,)), ((), ())), preferred_element_type=f32)


def forward(v):
    s0, s1, d0, d1 = v[0] + v[4], v[1] + v[3], v[0] - v[4], v[1] - v[3]
    out = [None] * 5
    for i in range(2):
        even = (
            float((D[i, 0] + D[i, 4]) / 2) * s0
            + float((D[i, 1] + D[i, 3]) / 2) * s1
            + float(D[i, 2]) * v[2]
        )
        odd = float((D[i, 0] - D[i, 4]) / 2) * d0 + float((D[i, 1] - D[i, 3]) / 2) * d1
        out[i] = even + odd
        out[4 - i] = odd - even
    out[2] = float(D[2, 0]) * d0 + float(D[2, 1]) * d1
    return out


def backward(h):
    s0, s1, d0, d1 = h[0] + h[4], h[1] + h[3], h[0] - h[4], h[1] - h[3]
    out = [None] * 5
    for p in range(2):
        even = (
            float((D[0, p] + D[4, p]) / 2) * s0
            + float((D[1, p] + D[3, p]) / 2) * s1
            + float(D[2, p]) * h[2]
        )
        odd = float((D[0, p] - D[4, p]) / 2) * d0 + float((D[1, p] - D[3, p]) / 2) * d1
        out[p] = even + odd
        out[4 - p] = odd - even
    out[2] = float(D[0, 2]) * d0 + float(D[1, 2]) * d1
    return out


def body(
    n_surf,
    n_depth,
    wave_hbm,
    adj_hbm,
    cell_hbm,
    elem_hbm,
    brick_hbm,
    count_hbm,
    density_hbm,
    modulus_hbm,
    scale_hbm,
    wave_old_hbm,
    adj_old_hbm,
    source_hbm,
    adj_source_hbm,
    wave_out,
    adj_out,
    brick_out,
    next_ref,
    blocks_ref,
    bricks,
    fields,
    cell_ref,
    elem_ref,
    brick_ref,
    count_ref,
    density_ref,
    modulus_ref,
    scale_ref,
    fold_ref,
    spread_ref,
    old,
    driven,
    halo_a,
    halo_c,
    halo_d,
    stage_a,
    stage_c,
    lhs,
    values,
    stiff,
    product,
    forces,
    folded,
    mass_lhs,
    mass_fold,
    mass_sum,
    face_a,
    face_c,
    face_d,
    got_a,
    got_c,
    got_d,
    write_sem,
    load_sem,
    send_sem,
    recv_sem,
):
    s = lax.axis_index("surf")
    d = lax.axis_index("depth")
    above_s, above_d = s < n_surf - 1, d < n_depth - 1
    below_s, below_d = s > 0, d > 0
    above_both, below_both = above_s & above_d, below_s & below_d
    up = ((s + 1, d, above_s), (s, d + 1, above_d), (s + 1, d + 1, above_both))
    down = ((s - 1, d, below_s), (s, d - 1, below_d), (s - 1, d - 1, below_both))

    first, second = pl.ds(0, 4 * PLANE), pl.ds(4 * PLANE, 4 * PLANE)
    moves = [
        (wave_hbm, fields.at[first]),
        (adj_hbm, fields.at[second]),
        (cell_hbm, cell_ref),
        (density_hbm, density_ref),
        (modulus_hbm, modulus_ref),
        (scale_hbm, scale_ref),
        (elem_hbm, elem_ref),
        (brick_hbm, brick_ref),
        (count_hbm, count_ref),
        (wave_old_hbm, old.at[first]),
        (adj_old_hbm, old.at[second]),
        (source_hbm, driven.at[first]),
        (adj_source_hbm, driven.at[second]),
    ]
    loads = [
        pltpu.make_async_copy(source, target, load_sem.at[k])
        for k, (source, target) in enumerate(moves)
    ]
    for load in loads:
        load.start()
    barrier = pltpu.get_barrier_semaphore()
    for to_s, to_d, there in up + down:

        @pl.when(there)
        def _():
            pl.semaphore_signal(barrier, inc=1, device_id=(to_s, to_d), device_id_type=MESH)

    fill_tables(spread_ref, fold_ref)
    for load in loads[:2]:
        load.wait()
    for c in range(NODES_C):
        stage_a[c * 8 : c * 8 + 8, :] = fields[pl.ds(c, 8, stride=PLANE), :]
    for a in range(NODES_A):
        stage_c[a * 8 : a * 8 + 8, :] = fields[pl.ds(a * NODES_C, 8, stride=PLANE), :]
    peers = sum(there.astype(jnp.int32) for _, _, there in up + down)
    pl.semaphore_wait(barrier, peers)

    def remote(source, target, k, to):
        return pltpu.make_async_remote_copy(
            src_ref=source,
            dst_ref=target,
            send_sem=send_sem.at[k],
            recv_sem=recv_sem.at[k],
            device_id=(to[0], to[1]),
            device_id_type=MESH,
        )

    halos = [
        remote(stage_a, halo_a, 0, down[0]),
        remote(stage_c, halo_c, 1, down[1]),
        remote(stage_a.at[pl.ds(0, 8)], halo_d, 2, down[2]),
    ]
    for copy, (_, _, there) in zip(halos, down):

        @pl.when(there)
        def _():
            copy.start()

    for load in loads[2:9]:
        load.wait()
    rows = lax.broadcasted_iota(jnp.int32, (256, 256), 0)
    placing = jnp.where(cell_ref[0:1, :] == rows, 1.0, 0.0).astype(bf16)

    def to_cells(ref):
        high, low = two_terms(ref[...])
        return dot_rows(high, placing) + dot_rows(low, placing)

    scale = jnp.concatenate([scale_ref[0:125, :]] * 2, axis=1)
    density = to_cells(density_ref) * scale
    modulus = to_cells(modulus_ref) * scale
    pad = jnp.zeros((3, 256), f32)
    density = jnp.concatenate([density, pad], axis=0)
    modulus = jnp.concatenate([modulus, pad], axis=0)
    expand = ones_where(iota((1024, 128), 0) >> 3 == iota((1024, 128), 1))
    stiff[...] = dot_right(expand, density)
    mass_row, node_lane = iota((48, 128), 0), iota((48, 128), 1)
    select = jnp.concatenate(
        [
            ones_where(5 * (mass_row - 20 * ea) + r == node_lane)
            for r in range(5)
            for ea in range(2)
        ],
        axis=0,
    )
    picked = dot_right(select, modulus)
    for r in range(5):
        mass_lhs[:, r * 128 : (r + 1) * 128] = (
            picked[r * 96 : r * 96 + 48, 0:128] + picked[r * 96 + 48 : r * 96 + 96, 128:256]
        )
    mass_fold[...] = dot_left(mass_lhs[...], fold_ref[...])
    for a in range(NODES_A + 1):
        for ec in range(4):
            lanes = slice(ec * 128, ec * 128 + 128)
            mass_sum[a * 24 + 4 * ec : a * 24 + 4 * ec + 4, :] = mass_fold[a * 5 : a * 5 + 4, lanes]
        for ec in range(4):
            lanes = slice(ec * 128, ec * 128 + 128)
            tail = mass_fold[a * 5 + 4 : a * 5 + 5, lanes]
            row = a * 24 + 4 * ec + 4
            if ec < 3:
                mass_sum[row : row + 1, :] += tail
            else:
                mass_sum[row : row + 1, :] = tail

    slots = lax.broadcasted_iota(jnp.int32, (1, 256), 1)
    digit_rows = lax.broadcasted_iota(jnp.int32, (16, 256), 0)
    digits = jnp.zeros((16, 256), f32)
    for t in range(4):
        live = slots < count_ref[0:1, t : t + 1]
        number = jnp.where(live, brick_ref[t : t + 1, :] + 1, 0)
        pair = jnp.where(
            digit_rows == 2 * t,
            number >> 5,
            jnp.where(digit_rows == 2 * t + 1, number & 31, 0),
        )
        listed = jnp.where(elem_ref[t : t + 1, :] == rows, 1.0, 0.0).astype(bf16)
        digits = digits + dot_rows(pair.astype(f32).astype(bf16), listed)
    digits = dot_rows(digits.astype(bf16), placing)
    for ea in range(2):
        blocks_ref[0, ea, 128:144, :] = digits[:, ea * 128 : ea * 128 + 128]

    zeros = jnp.zeros((8, 128), f32)
    lhs[360:384, :] = jnp.zeros((24, 512), f32)
    forces[200:384, :] = jnp.zeros((184, 640), f32)

    def place(a, c, tile):
        ec, q = c // 4, c % 4
        if ec < 4:
            lhs[pl.ds(pl.multiple_of((a * 5 + q) * 8, 8), 8), ec * 128 : ec * 128 + 128] = tile
        if q == 0 and ec > 0:
            lhs[pl.ds(pl.multiple_of((a * 5 + 4) * 8, 8), 8), (ec - 1) * 128 : ec * 128] = tile

    def place_plane(a, carry):
        for c in range(NODES_C):
            place(a, c, fields[pl.ds(a * NODES_C + c, 8, stride=PLANE), :])
        return carry

    lax.fori_loop(0, NODES_A, place_plane, 0)

    for buffer, (_, _, there) in zip((halo_a, halo_c, halo_d), up):

        @pl.when(jnp.logical_not(there))
        def _():
            buffer[...] = jnp.zeros(buffer.shape, f32)

    for copy, (_, _, there) in zip(halos, down):

        @pl.when(there)
        def _():
            copy.wait_send()

    for copy, (_, _, there) in zip(halos, up):

        @pl.when(there)
        def _():
            copy.wait_recv()

    for c in range(NODES_C):
        place(8, c, halo_a[c * 8 : c * 8 + 8, :])
    for a in range(NODES_A):
        place(a, 16, halo_c[a * 8 : a * 8 + 8, :])
    place(8, 16, halo_d[...])

    values[...] = dot_left(lhs[...], spread_ref[...])
    product[1000:1024, :] = jnp.zeros((24, 256), f32)

    gather = ones_where(iota((128, 1024), 1) >> 3 == iota((128, 1024), 0), 0.5)

    def mates(g):
        return g * pltpu.roll(g, 4, 0)

    def eight(k):
        return pl.ds(pl.multiple_of(k * 8, 8), 8)

    def block_send(ea, k):
        own = 1 if k == 2 else 0
        return remote(
            blocks_ref.at[own, ea], blocks_ref.at[1 + k, ea], 3 + 3 * ea + k, up[1 if k else 0]
        )

    for k in range(3):

        @pl.when(jnp.logical_not(down[k][2]))
        def _():
            blocks_ref[1 + k] = jnp.zeros((2, BLOCK_ROWS, 128), f32)

    relayed = below_s & above_d

    def relay(ea):
        @pl.when(below_s)
        def _():
            block_send(ea, 0).wait_recv()

        @pl.when(relayed)
        def _():
            block_send(ea, 2).start()

    for ea in range(2):
        half = slice(ea * 128, ea * 128 + 128)

        def plane(p, carry):
            v = [
                [
                    values[eight((4 * ea + p) * 5 + q), r * 128 : r * 128 + 128]
                    for r in range(5)
                ]
                for q in range(5)
            ]
            k = [[stiff[eight(p * 25 + q * 5 + r), half] for r in range(5)] for q in range(5)]
            pair = [[None] * 5 for _ in range(5)]
            force = [[None] * 5 for _ in range(5)]
            for r in range(5):
                g = forward([v[q][r] for q in range(5)])
                f = backward([k[q][r] * g[q] for q in range(5)])
                for q in range(5):
                    pair[q][r] = mates(g[q])
                    force[q][r] = f[q]
            for q in range(5):
                g = forward(v[q])
                f = backward([k[q][r] * g[r] for r in range(5)])
                for r in range(5):
                    product[eight(p * 25 + q * 5 + r), half] = pair[q][r] + mates(g[r])
                    at = eight((4 * ea + p) * 5 + q), slice(r * 128, r * 128 + 128)
                    total = force[q][r] + f[r]
                    forces[at] = total if ea == 0 else forces[at] + total
            return carry

        lax.fori_loop(0, 5, plane, 0)

        def line(q, carry):
            for r in range(5):
                lanes = slice(r * 128, r * 128 + 128)
                g = forward([values[eight((4 * ea + p) * 5 + q), lanes] for p in range(5)])
                f = backward([stiff[eight(p * 25 + q * 5 + r), half] * g[p] for p in range(5)])
                for p in range(5):
                    product[eight(p * 25 + q * 5 + r), half] += mates(g[p])
                    forces[eight((4 * ea + p) * 5 + q), lanes] += f[p]
            return carry

        lax.fori_loop(0, 5, line, 0)

        blocks_ref[0, ea, 0:128, :] = dot_right(gather, product[:, half]) * (
            -time_step * scale_ref[...]
        )
        for k in range(2):

            @pl.when(up[k][2])
            def _():
                block_send(ea, k).start()

    folded[...] = dot_left(forces[...], fold_ref[...])

    def node(a, c):
        ec, q = c // 4, c % 4
        out = None
        if ec < 4:
            out = folded[eight(a * 5 + q), ec * 128 : ec * 128 + 128]
        if q == 0 and ec > 0:
            tail = folded[eight(a * 5 + 4), (ec - 1) * 128 : ec * 128]
            out = tail if out is None else out + tail
        return out

    for c in range(NODES_C):
        face_a[c * 8 : c * 8 + 8, :] = node(8, c)
    face_a[128:144, :] = mass_sum[192:208, :]
    for a in range(NODES_A):
        face_c[a * 8 : a * 8 + 8, :] = node(a, 16)
        face_c[64 + a : 65 + a, :] = mass_sum[a * 24 + 16 : a * 24 + 17, :]
    face_d[0:8, :] = node(8, 16)
    face_d[8:16, :] = jnp.broadcast_to(mass_sum[208:209, :], (8, 128))
    faces = [
        remote(face_a, got_a, 9, up[0]),
        remote(face_c, got_c, 10, up[1]),
        remote(face_d, got_d, 11, up[2]),
    ]
    for copy, (_, _, there) in zip(faces, up):

        @pl.when(there)
        def _():
            copy.start()

    for buffer, (_, _, there) in zip((got_a, got_c, got_d), down):

        @pl.when(jnp.logical_not(there))
        def _():
            buffer[...] = jnp.zeros(buffer.shape, f32)

    relay(0)

    def arrived(k):
        for ea in range(2):

            @pl.when(down[k][2])
            def _():
                block_send(ea, k).wait_recv()

    def into_bricks(t):
        block = jnp.concatenate([blocks_ref[t, 0], blocks_ref[t, 1]], axis=1)
        stacked = jnp.concatenate(two_terms(block[0:128]), axis=0)
        row = 128 + 2 * t
        target = block[row : row + 1] * 32.0 + block[row + 1 : row + 2] - 1.0
        for n in range(bricks.shape[1] // 256):
            part = dot_rows(stacked, ones_where(target == (rows + n * 256).astype(f32)))
            part = part[0:125] + part[128:253]
            lanes = slice(n * 256, n * 256 + 256)
            if t == 0:
                bricks[:, lanes] = part
            else:
                bricks[:, lanes] += part

    def write_plane(a, carry):
        for c in range(1, NODES_C):
            next_ref[pl.ds(a * NODES_C + c, 8, stride=PLANE), :] = node(a, c)
        return carry

    lax.fori_loop(1, NODES_A, write_plane, 0)
    into_bricks(0)
    for load in loads[9:]:
        load.wait()
    relay(1)
    into_bricks(1)
    arrived(1)
    into_bricks(2)

    for copy, (_, _, there) in zip(faces, up):

        @pl.when(there)
        def _():
            copy.wait_send()

    for copy, (_, _, there) in zip(faces, down):

        @pl.when(there)
        def _():
            copy.wait_recv()

    for c in range(1, NODES_C):
        next_ref[pl.ds(c, 8, stride=PLANE), :] = node(0, c) + got_a[c * 8 : c * 8 + 8, :]
    for a in range(1, NODES_A):
        next_ref[pl.ds(a * NODES_C, 8, stride=PLANE), :] = (
            node(a, 0) + got_c[a * 8 : a * 8 + 8, :]
        )
    next_ref[pl.ds(0, 8, stride=PLANE), :] = (
        node(0, 0) + got_a[0:8, :] + got_c[0:8, :] + got_d[0:8, :]
    )
    mass_sum[0:16, :] += got_a[128:144, :]
    for a in range(NODES_A):
        mass_sum[a * 24 : a * 24 + 1, :] += got_c[64 + a : 65 + a, :]
    mass_sum[0:1, :] += got_d[8:9, :]
    inverse = jnp.concatenate([mass_sum[a * 24 : a * 24 + 16, :] for a in range(NODES_A)], axis=0)
    inverse = time_step * time_step / inverse

    def update(x, carry):
        at = pl.ds(pl.multiple_of(x * PLANE, PLANE), PLANE)
        next_ref[at, :] = (
            2.0 * fields[at, :] - old[at, :] + (driven[at, :] - next_ref[at, :]) * inverse
        )
        return carry

    lax.fori_loop(0, 8, update, 0)

    writes = [
        pltpu.make_async_copy(next_ref.at[first], wave_out, write_sem.at[0]),
        pltpu.make_async_copy(next_ref.at[second], adj_out, write_sem.at[1]),
        pltpu.make_async_copy(bricks, brick_out, write_sem.at[2]),
    ]
    for write in writes[:2]:
        write.start()
    arrived(2)
    into_bricks(3)
    writes[2].start()
    for ea in range(2):
        for k, sent in enumerate((above_s, above_d, relayed)):

            @pl.when(sent)
            def _():
                block_send(ea, k).wait_send()

    for write in writes:
        write.wait()


def per_device(
    n_surf,
    n_depth,
    wave_now,
    wave_old,
    adj_now,
    adj_old,
    source,
    adj_source,
    inv_density,
    inv_modulus,
    element_cell,
    send_elem,
    send_brick,
    send_count,
):
    scale = cubature_rows()
    anywhere = pl.BlockSpec(memory_space=pl.ANY)

    def flat(x):
        return x.reshape(4 * PLANE, 128)

    operands = [
        flat(wave_now),
        flat(adj_now),
        element_cell,
        send_elem[0],
        send_brick[0],
        send_count,
        inv_density,
        inv_modulus,
        jnp.asarray(scale, f32),
        flat(wave_old),
        flat(adj_old),
        flat(source),
        flat(adj_source),
    ]
    held = [pltpu.VMEM(x.shape, x.dtype) for x in operands[2:9]]
    half = jax.ShapeDtypeStruct((4 * PLANE, 128), f32)
    results = (half, half, jax.ShapeDtypeStruct((125, 1024), f32))
    wave_next, adj_next, brick_kernel = pl.pallas_call(
        functools.partial(body, n_surf, n_depth),
        out_shape=results,
        in_specs=[anywhere] * len(operands),
        out_specs=(anywhere,) * 3,
        scratch_shapes=[
            pltpu.VMEM((8 * PLANE, 128), f32),
            pltpu.VMEM((4, 2, BLOCK_ROWS, 128), f32),
            pltpu.VMEM((125, 1024), f32),
            pltpu.VMEM((8 * PLANE, 128), f32),
        ]
        + held
        + [
            pltpu.VMEM((640, 512), bf16),
            pltpu.VMEM((512, 640), bf16),
            pltpu.VMEM((8 * PLANE, 128), f32),
            pltpu.VMEM((8 * PLANE, 128), f32),
            pltpu.VMEM((128, 128), f32),
            pltpu.VMEM((64, 128), f32),
            pltpu.VMEM((8, 128), f32),
            pltpu.VMEM((128, 128), f32),
            pltpu.VMEM((64, 128), f32),
            pltpu.VMEM((384, 512), f32),
            pltpu.VMEM((384, 640), f32),
            pltpu.VMEM((1024, 256), f32),
            pltpu.VMEM((1024, 256), f32),
            pltpu.VMEM((384, 640), f32),
            pltpu.VMEM((384, 512), f32),
            pltpu.VMEM((48, 640), f32),
            pltpu.VMEM((48, 512), f32),
            pltpu.VMEM((216, 128), f32),
            pltpu.VMEM((FACE_A, 128), f32),
            pltpu.VMEM((FACE_C, 128), f32),
            pltpu.VMEM((FACE_D, 128), f32),
            pltpu.VMEM((FACE_A, 128), f32),
            pltpu.VMEM((FACE_C, 128), f32),
            pltpu.VMEM((FACE_D, 128), f32),
            pltpu.SemaphoreType.DMA((3,)),
            pltpu.SemaphoreType.DMA((len(operands),)),
            pltpu.SemaphoreType.DMA((12,)),
            pltpu.SemaphoreType.DMA((12,)),
        ],
        compiler_params=pltpu.CompilerParams(
            collective_id=0, has_side_effects=True, vmem_limit_bytes=60 * 1024 * 1024
        ),
    )(*operands)
    shape = wave_now.shape
    return wave_next.reshape(shape), adj_next.reshape(shape), brick_kernel


def solution(mesh):
    field = P(None, "surf", "depth", None)
    column = P(None, ("surf", "depth"))
    placed = (field,) * 6 + (
        column,
        column,
        P(("surf", "depth"), None),
        P(("surf", "depth"), None, None),
        P(("surf", "depth"), None, None),
        P(("surf", "depth"), None),
    )
    return jax.shard_map(
        functools.partial(per_device, mesh.shape["surf"], mesh.shape["depth"]),
        mesh=mesh,
        in_specs=placed,
        out_specs=(field, field, column),
        check_vma=False,
    )
```
